32 devices in a mesh: gy: 8 (over z, core), gx: 4 (over y, x).
Axes of the slice: x: 2, y: 2, z: 4, core: 2. Of those that a mesh axis runs over, the one named last changes fastest.
Arguments:
- tokens: bfloat16 [256, 512, 256], P('gy', 'gx'), may hold values from -40 to 40
- cotangent: bfloat16 [256, 512, 256], P('gy', 'gx'), may hold values from -6 to 6
- norm1_gain: float32 [256], replicated, may hold values from 0.25 to 1.75
- w_qkv: bfloat16 [256, 768], replicated, may hold values from -0.375 to 0.375
- w_out: bfloat16 [256, 256], replicated, may hold values from -0.375 to 0.375
- pos_bias: float32 [8, 64, 64], replicated, may hold values from -3.5 to 302
- norm2_gain: float32 [256], replicated, may hold values from 0.25 to 1.75
- w_up: bfloat16 [256, 1024], replicated, may hold values from -0.375 to 0.375
- w_down: bfloat16 [1024, 256], replicated, may hold values from -0.1875 to 0.1875
Outputs:
- mixed: bfloat16 [256, 512, 256], P('gy', 'gx')
- grad_tokens: bfloat16 [256, 512, 256], P('gy', 'gx')
- grad_qkv: float32 [256, 768], replicated
- grad_out: float32 [256, 256], replicated
The draws below stay inside these ranges and needn't reach their ends.
All inputs are finite; a program needn't handle non-finite values.
Results may differ from the reference program's by a relative error of at most 0.009.
Values may be sent and summed in bfloat16 or wider, within the bound.
A program may use at most 192 MiB of HBM per device.

```python
import math
import jax
import jax.numpy as jnp
from jax import lax

C = 256
HEADS = 8
FF = 1024
GRID = 8
ROWS = 256
COLS = 512


def draw_tokens(key, part):
    key = jax.random.fold_in(key, 11)
    base_key, row_key, chan_key = jax.random.split(key, 3)
    shape = (ROWS, COLS, C)
    base = jnp.clip(jax.random.normal(base_key, shape, jnp.float32), -4.0, 4.0)
    row_scale = jnp.exp(jax.random.uniform(row_key, (ROWS, COLS, 1), jnp.float32, math.log(0.3), math.log(3.0)))
    chan_scale = jnp.exp(jax.random.uniform(chan_key, (C,), jnp.float32, math.log(0.3), math.log(3.0)))
    return (base * row_scale * chan_scale).astype(jnp.bfloat16)


def draw_pos_bias(key, part):
    key = jax.random.fold_in(key, 23)
    keys = jax.random.split(key, 1)
    members = GRID * GRID
    shape = (HEADS, members, members)
    return jnp.clip(jax.random.normal(keys[0], shape, jnp.float32), -3.0, 3.0)


def steps_of(stream_key, shape, pieces, low, high):
    factor_of, own = 1.0, jax.random.fold_in(stream_key, 6)
    for axis_at, shards_of in pieces:
        heights = jnp.exp(jax.random.uniform(jax.random.fold_in(own, axis_at), (shards_of,), jnp.float32, low / len(pieces), high / len(pieces)))
        factor_of = factor_of * jnp.repeat(heights, shape[axis_at] // shards_of).reshape([-1 if axis == axis_at else 1 for axis in range(len(shape))])
    return factor_of


def centred(rng, dims, deviation, bound, pieces=(), held_as=jnp.bfloat16):
    array = jax.random.normal(rng, dims, jnp.float32) * deviation
    if len(pieces) > 0:
        array = steps_of(rng, dims, pieces, -0.22, 0.18) * array
    return jnp.clip(array, min=-bound, max=bound).astype(held_as)


def setup_inputs(seed: int = 0) -> dict:
    streams_of = jax.random.split(jax.random.key(seed), 10)
    return {
        "tokens": draw_tokens(jax.random.fold_in(streams_of[9], 71), 0),
        "cotangent": centred(streams_of[1], (ROWS, COLS, C), 1.0, 6.0, ((0, 8), (1, 4))),
        "norm1_gain": jnp.clip(1.0 + 0.15 * jax.random.normal(streams_of[2], (C,), jnp.float32), 0.25, 1.75),
        "w_qkv": centred(streams_of[3], (C, 3 * C), C ** -0.5, 0.375),
        "w_out": centred(streams_of[4], (C, C), C ** -0.5, 0.375),
        "pos_bias": draw_pos_bias(jax.random.fold_in(streams_of[9], 71), 0),
        "norm2_gain": jnp.clip(1.0 + 0.15 * jax.random.normal(streams_of[6], (C,), jnp.float32), 0.25, 1.75),
        "w_up": centred(streams_of[7], (C, FF), C ** -0.5, 0.375),
        "w_down": centred(streams_of[8], (FF, C), FF ** -0.5, 0.1875),
    }


EPSILON = 1e-05

def rounded(values):
    return lax.optimization_barrier(values.astype(jnp.bfloat16)).astype(jnp.float32)

def normalize(values, gain):
    wide = values.astype(jnp.float32)
    centre = lax.optimization_barrier(jnp.mean(wide, axis=-1, keepdims=True))
    shifted = wide - centre
    variance = lax.optimization_barrier(jnp.mean(shifted * shifted, axis=-1, keepdims=True))
    inverse = lax.rsqrt(variance + EPSILON)
    unit = shifted * inverse
    return (unit * gain, unit, inverse)

def feed_forward(attended, norm2_gain, w_up, w_down):
    normed_wide, unit, inverse = normalize(attended, norm2_gain)
    normed2 = normed_wide.astype(jnp.bfloat16)
    hidden = jax.nn.gelu(jnp.dot(normed2, w_up, preferred_element_type=jnp.float32)).astype(jnp.bfloat16)
    return (attended.astype(jnp.float32) + jnp.dot(hidden, w_down, preferred_element_type=jnp.float32)).astype(jnp.bfloat16)

def layer_block(x_rows, g_rows, norm1_gain, w_qkv, w_out, pos_bias, norm2_gain, w_up, w_down, groups):
    channels = x_rows.shape[-1]
    heads = pos_bias.shape[0]
    members = pos_bias.shape[1]
    width = channels // heads
    scale_factor = 1.0 / math.sqrt(width)
    normed_wide, unit, inverse = normalize(x_rows, norm1_gain)
    normed = normed_wide.astype(jnp.bfloat16)
    qkv = jnp.dot(normed, w_qkv, preferred_element_type=jnp.float32)
    split_qkv = rounded(qkv).reshape(groups, members, 3, heads, width)
    query = split_qkv[:, :, 0]
    keys = split_qkv[:, :, 1]
    values = split_qkv[:, :, 2]
    scores = jnp.einsum('nmhd,nkhd->nhmk', query, keys) * scale_factor + pos_bias[None]
    soft = jax.nn.softmax(scores, axis=-1)
    soft_low = rounded(soft)
    context = jnp.einsum('nhmk,nkhd->nmhd', soft_low, values).astype(jnp.bfloat16).reshape(groups * members, channels)
    attended = (x_rows.astype(jnp.float32) + jnp.dot(context, w_out, preferred_element_type=jnp.float32)).astype(jnp.bfloat16)
    mixed = feed_forward(attended, norm2_gain, w_up, w_down)
    d_context = jnp.dot(g_rows, w_out.T, preferred_element_type=jnp.float32).astype(jnp.bfloat16)
    d_wout = jnp.dot(context.T, g_rows, preferred_element_type=jnp.float32)
    d_ctx = d_context.astype(jnp.float32).reshape(groups, members, heads, width)
    d_soft = jnp.einsum('nmhd,nkhd->nhmk', d_ctx, values)
    d_scores = soft * (d_soft - lax.optimization_barrier(jnp.sum(soft * d_soft, axis=-1, keepdims=True)))
    d_scaled = rounded(d_scores * scale_factor)
    d_query = jnp.einsum('nhmk,nkhd->nmhd', d_scaled, keys)
    d_keys = jnp.einsum('nhmk,nmhd->nkhd', d_scaled, query)
    d_values = jnp.einsum('nhmk,nmhd->nkhd', soft_low, d_ctx)
    d_qkv = jnp.stack([d_query, d_keys, d_values], axis=2).astype(jnp.bfloat16).reshape(groups * members, 3 * channels)
    d_wqkv = jnp.dot(normed.T, d_qkv, preferred_element_type=jnp.float32)
    d_normed = jnp.dot(d_qkv, w_qkv.T, preferred_element_type=jnp.float32)
    d_unit = d_normed * norm1_gain
    d_x = inverse * (d_unit - lax.optimization_barrier(jnp.mean(d_unit, axis=-1, keepdims=True)) - unit * lax.optimization_barrier(jnp.mean(d_unit * unit, axis=-1, keepdims=True)))
    grad_rows = (g_rows.astype(jnp.float32) + d_x).astype(jnp.bfloat16)
    return (mixed, grad_rows, d_wqkv, d_wout)

def reference(tokens, cotangent, norm1_gain, w_qkv, w_out, pos_bias, norm2_gain, w_up, w_down):
    rows, cols, channels = tokens.shape
    stride_r = rows // GRID
    stride_c = cols // GRID
    members = GRID * GRID
    total = stride_r * stride_c
    block = math.gcd(total, 64)
    count = total // block

    def group(values):
        arranged = values.reshape(GRID, stride_r, GRID, stride_c, channels).transpose(1, 3, 0, 2, 4)
        return arranged.reshape(count, block * members, channels)

    def ungroup(values):
        arranged = values.reshape(stride_r, stride_c, GRID, GRID, channels).transpose(2, 0, 3, 1, 4)
        return arranged.reshape(rows, cols, channels)

    def step_block(carry, pair):
        mixed_rows, grad_rows, d_wqkv, d_wout = layer_block(pair[0], pair[1], norm1_gain, w_qkv, w_out, pos_bias, norm2_gain, w_up, w_down, block)
        return ((carry[0] + d_wqkv, carry[1] + d_wout), (mixed_rows, grad_rows))
    start = (jnp.zeros((channels, 3 * channels), jnp.float32), jnp.zeros((channels, channels), jnp.float32))
    sums, outputs = lax.scan(step_block, start, (group(tokens), group(cotangent)))
    factor = 1.0 / math.sqrt(rows * cols)
    return (ungroup(outputs[0]), ungroup(outputs[1]), sums[0] * factor, sums[1] * factor)
```

```python
import functools
import math

import jax
import jax.numpy as jnp
from jax import lax
from jax.experimental import pallas as pl
from jax.experimental.pallas import tpu as pltpu
from jax.sharding import PartitionSpec as P

GRID = 8
MEMBERS = GRID * GRID
EPSILON = 1e-05
BATCH = 16
MESH = pl.DeviceIdType.MESH
F32 = jnp.float32
BF16 = jnp.bfloat16


def dot(a, b, da=1, db=0):
    return lax.dot_general(a, b, (((da,), (db,)), ((), ())), preferred_element_type=F32)


def unit_of(wide):
    centre = jnp.mean(wide, axis=-1, keepdims=True)
    shifted = wide - centre
    variance = jnp.mean(shifted * shifted, axis=-1, keepdims=True)
    inverse = lax.rsqrt(variance + EPSILON)
    return shifted * inverse, inverse


def chunk_work(block, result, weights, acc, work, heads):
    gain1, w_qkv, w_out, bias, gain2, w_up, w_down, mask = weights
    wide, xg, gg, normed, qkv, dctx, ctx, dqkv = work
    channels = xg.shape[-1]
    rows = BATCH * MEMBERS
    scale = 1.0 / math.sqrt(channels // heads)
    half = 128

    for tensor, kept in ((0, xg), (1, gg)):
        value = block[tensor].astype(F32).reshape(rows, channels)
        for part in range(channels // half):
            wide[part] = value[:, part * half : (part + 1) * half]
        for group in range(BATCH):
            for part in range(channels // half):
                kept[group * MEMBERS : (group + 1) * MEMBERS, part * half : (part + 1) * half] = wide[
                    part, pl.ds(group, MEMBERS, stride=BATCH), :
                ].astype(BF16)

    step = 256

    def before(index, carry):
        at = pl.ds(pl.multiple_of(index * step, step), step)
        unit, inverse = unit_of(xg[at, :].astype(F32))
        low = (unit * gain1[...]).astype(BF16)
        normed[at, :] = low
        qkv[at, :] = dot(low, w_qkv[...]).astype(BF16)
        dctx[at, :] = dot(gg[at, :], w_out[...], 1, 1).astype(BF16)
        return carry

    lax.fori_loop(0, rows // step, before, 0)

    def one_group(at):
        query = qkv[at, 0:channels]
        keys = qkv[at, channels : 2 * channels]
        values = qkv[at, 2 * channels : 3 * channels]
        spread = mask[...]
        query_wide = jnp.concatenate([query] * heads, axis=0) * spread
        d_wide = jnp.concatenate([dctx[at, :]] * heads, axis=0) * spread
        scores = dot(keys, query_wide, 1, 1) * scale + bias[...]
        top = jnp.max(scores, axis=0, keepdims=True)
        raised = jnp.exp(scores - top)
        probs = raised / jnp.sum(raised, axis=0, keepdims=True)
        low = probs.astype(BF16)
        d_probs = dot(values, d_wide, 1, 1)
        inner = jnp.sum(probs * d_probs, axis=0, keepdims=True)
        d_scaled = (probs * (d_probs - inner) * scale).astype(BF16)

        def gathered(left, right):
            full = dot(left, right, 0, 0)
            lane = lax.broadcasted_iota(jnp.int32, (MEMBERS, channels), 1) // (channels // heads)
            total = full[0:MEMBERS]
            for head in range(1, heads):
                total = jnp.where(lane == head, full[head * MEMBERS : (head + 1) * MEMBERS], total)
            return total

        ctx[at, :] = gathered(low, values).astype(BF16)
        dqkv[at, 0:channels] = gathered(d_scaled, keys).astype(BF16)
        dqkv[at, channels : 2 * channels] = dot(d_scaled, query_wide).astype(BF16)
        dqkv[at, 2 * channels : 3 * channels] = dot(low, d_wide).astype(BF16)

    def attend(index, carry):
        for inner in range(2):
            one_group(pl.ds(pl.multiple_of((2 * index + inner) * MEMBERS, MEMBERS), MEMBERS))
        return carry

    lax.fori_loop(0, BATCH // 2, attend, 0)

    acc[:, 0 : 3 * channels] += dot(normed[...], dqkv[...], 0, 0)
    acc[:, 3 * channels : 4 * channels] += dot(ctx[...], gg[...], 0, 0)

    def spread_out(index, value):
        groups = step // MEMBERS
        for local in range(groups):
            for part in range(channels // half):
                wide[part, pl.ds(index * groups + local, MEMBERS, stride=BATCH), :] = value[
                    local * MEMBERS : (local + 1) * MEMBERS, part * half : (part + 1) * half
                ]

    def finish(tensor):
        value = jnp.concatenate([wide[part] for part in range(channels // half)], axis=1)
        result[tensor] = value.reshape(MEMBERS, BATCH, channels).astype(BF16)

    def forward(index, carry):
        at = pl.ds(pl.multiple_of(index * step, step), step)
        attended = (xg[at, :].astype(F32) + dot(ctx[at, :], w_out[...])).astype(BF16).astype(F32)
        unit, inverse = unit_of(attended)
        low = (unit * gain2[...]).astype(BF16)
        hidden = jax.nn.gelu(dot(low, w_up[...])).astype(BF16)
        spread_out(index, attended + dot(hidden, w_down[...]))
        return carry

    lax.fori_loop(0, rows // step, forward, 0)
    finish(0)

    def backward(index, carry):
        at = pl.ds(pl.multiple_of(index * step, step), step)
        unit, inverse = unit_of(xg[at, :].astype(F32))
        d_unit = dot(dqkv[at, :], w_qkv[...], 1, 1) * gain1[...]
        d_x = inverse * (
            d_unit
            - jnp.mean(d_unit, axis=-1, keepdims=True)
            - unit * jnp.mean(d_unit * unit, axis=-1, keepdims=True)
        )
        spread_out(index, gg[at, :].astype(F32) + d_x)
        return carry

    lax.fori_loop(0, rows // step, backward, 0)
    finish(1)


def kernel(
    plan,
    tokens, cotangent, gain1, w_qkv, w_out, bias, gain2, w_up, w_down, mask,
    mixed, grad_tokens, sums,
    inbox, outbox, acc, wide, xg, gg, normed, qkv, dctx, ctx, dqkv, parts, shares, share, whole,
    sent_in, sent_out, sent_sum, sent_share, chunk_sem, mixed_sem, grad_sem, sum_sem, share_sem,
):
    row_devices, column_devices, row_part, extra, members, splits, strip, per_block, heads = plan
    count = row_devices * column_devices
    gy = lax.axis_index("gy")
    gx = lax.axis_index("gx")
    me = gy * column_devices + gx

    def place(device):
        return device // column_devices, device % column_devices

    def home(device):
        row, column = place(device)
        return row * row_part + column // splits, (column % splits) * strip

    def seat(device):
        row, column = place(device)
        return (row // extra) * GRID + column * members, row % extra

    def peers(body):
        def step(index, carry):
            device = (me + index) % count
            body(index, device, place(device))
            return carry

        lax.fori_loop(1, count, step, 0)

    barrier = pltpu.get_barrier_semaphore()
    peers(lambda index, device, at: pl.semaphore_signal(barrier, inc=1, device_id=at, device_id_type=MESH))
    pl.semaphore_wait(barrier, count - 1)

    my_member, my_extra = seat(me)
    my_row, my_column = home(me)

    def send_block(piece, _):
        chunk = my_extra * per_block + piece
        span = pl.ds(my_member, members)

        def source(device, array):
            row, column = home(device)
            return array.at[row, :, pl.ds(pl.multiple_of(column + piece * BATCH, BATCH), BATCH), :]

        for tensor, array in ((0, tokens), (1, cotangent)):
            pltpu.make_async_copy(
                source(me, array), inbox.at[chunk, tensor, span], chunk_sem.at[chunk]
            ).start()

        def to_peer(index, device, at):
            for tensor, array in ((0, tokens), (1, cotangent)):
                pltpu.make_async_remote_copy(
                    src_ref=source(device, array),
                    dst_ref=inbox.at[chunk, tensor, span],
                    send_sem=sent_in.at[index],
                    recv_sem=chunk_sem.at[chunk],
                    device_id=at,
                    device_id_type=MESH,
                ).start()

        peers(to_peer)
        return _

    lax.fori_loop(0, per_block, send_block, 0)
    acc[...] = jnp.zeros_like(acc)
    weights = (gain1, w_qkv, w_out, bias, gain2, w_up, w_down, mask)
    work = (wide, xg, gg, normed, qkv, dctx, ctx, dqkv)

    def one_chunk(chunk, _):
        pltpu.make_async_copy(inbox.at[chunk], inbox.at[chunk], chunk_sem.at[chunk]).wait()
        chunk_work(inbox.at[chunk], outbox.at[chunk], weights, acc, work, heads)
        part = chunk // per_block
        piece = chunk % per_block
        column = pl.ds(pl.multiple_of(my_column + piece * BATCH, BATCH), BATCH)
        targets = ((0, mixed, mixed_sem), (1, grad_tokens, grad_sem))

        def keep():
            for tensor, array, sem in targets:
                pltpu.make_async_copy(
                    outbox.at[chunk, tensor, pl.ds(my_member, members)], array.at[my_row, :, column, :], sem
                ).start()

        def to_peer(index, device, at):
            member, its = seat(device)

            def send():
                for tensor, array, sem in targets:
                    pltpu.make_async_remote_copy(
                        src_ref=outbox.at[chunk, tensor, pl.ds(member, members)],
                        dst_ref=array.at[my_row, :, column, :],
                        send_sem=sent_out.at[index],
                        recv_sem=sem,
                        device_id=at,
                        device_id_type=MESH,
                    ).start()

            if extra == 1:
                send()
            else:
                pl.when(its == part)(send)

        if extra == 1:
            keep()
        else:
            pl.when(my_extra == part)(keep)
        peers(to_peer)
        return _

    lax.fori_loop(0, extra * per_block, one_chunk, 0)

    height, width = share.shape
    across = acc.shape[1] // width
    for device in range(count):
        top, left = device // across * height, device % across * width
        parts[device] = acc[top : top + height, left : left + width].astype(BF16)
    pltpu.make_async_copy(parts.at[me], shares.at[me], sum_sem).start()
    peers(
        lambda index, device, at: pltpu.make_async_remote_copy(
            src_ref=parts.at[device],
            dst_ref=shares.at[me],
            send_sem=sent_sum.at[index],
            recv_sem=sum_sem,
            device_id=at,
            device_id_type=MESH,
        ).start()
    )
    pltpu.make_async_copy(shares, shares, sum_sem).wait()
    share[...] = jnp.sum(shares[...].astype(F32), axis=0).astype(BF16)
    pltpu.make_async_copy(share, whole.at[me], share_sem).start()
    peers(
        lambda index, device, at: pltpu.make_async_remote_copy(
            src_ref=share,
            dst_ref=whole.at[me],
            send_sem=sent_share.at[index],
            recv_sem=share_sem,
            device_id=at,
            device_id_type=MESH,
        ).start()
    )
    pltpu.make_async_copy(whole, whole, share_sem).wait()
    for device in range(count):
        top, left = device // across * height, device % across * width
        sums[top : top + height, left : left + width] = whole[device].astype(F32)

    def drain(index, device, at):
        moved = inbox.at[pl.ds(0, per_block), :, pl.ds(0, members)]
        pltpu.make_async_copy(moved, moved, sent_in.at[index]).wait()
        pltpu.make_async_copy(moved, moved, sent_out.at[index]).wait()
        pltpu.make_async_copy(share, share, sent_sum.at[index]).wait()
        pltpu.make_async_copy(share, share, sent_share.at[index]).wait()

    peers(drain)
    pltpu.make_async_copy(mixed, mixed, mixed_sem).wait()
    pltpu.make_async_copy(grad_tokens, grad_tokens, grad_sem).wait()


def local(tokens, cotangent, norm1_gain, w_qkv, w_out, pos_bias, norm2_gain, w_up, w_down):
    tile_rows, tile_cols, channels = tokens.shape
    row_devices = lax.axis_size("gy")
    column_devices = lax.axis_size("gx")
    count = row_devices * column_devices
    heads, nodes = pos_bias.shape[:2]
    row_part = tile_rows // row_devices
    extra = row_devices // GRID
    members = GRID // column_devices
    stride = tile_cols // members
    splits = column_devices // row_part
    strip = stride // splits
    per_block = strip // BATCH
    chunks = extra * per_block
    plan = (row_devices, column_devices, row_part, extra, members, splits, strip, per_block, heads)
    factor = 1.0 / math.sqrt(tile_rows * tile_cols * count)
    shape = (tile_rows, members, stride, channels)
    rows = BATCH * MEMBERS
    bias = pos_bias.transpose(2, 0, 1).reshape(nodes, heads * nodes)
    head_of_row = jnp.arange(heads * nodes)[:, None] // nodes
    head_of_lane = jnp.arange(channels)[None, :] // (channels // heads)
    mask = (head_of_row == head_of_lane).astype(BF16)
    width = 4 * channels * channels // (16 * count)
    anywhere = pl.BlockSpec(memory_space=pl.ANY)
    vmem = pl.BlockSpec(memory_space=pltpu.VMEM)
    dma = pltpu.SemaphoreType.DMA
    box = (chunks, 2, MEMBERS, BATCH, channels)
    mixed, grad_tokens, sums = pl.pallas_call(
        functools.partial(kernel, plan),
        out_shape=(
            jax.ShapeDtypeStruct(shape, BF16),
            jax.ShapeDtypeStruct(shape, BF16),
            jax.ShapeDtypeStruct((channels, 4 * channels), F32),
        ),
        in_specs=[anywhere, anywhere] + [vmem] * 8,
        out_specs=(anywhere, anywhere, vmem),
        scratch_shapes=[
            pltpu.VMEM(box, BF16),
            pltpu.VMEM(box, BF16),
            pltpu.VMEM((channels, 4 * channels), F32),
            pltpu.VMEM((channels // 128, rows, 128), F32),
            pltpu.VMEM((rows, channels), BF16),
            pltpu.VMEM((rows, channels), BF16),
            pltpu.VMEM((rows, channels), BF16),
            pltpu.VMEM((rows, 3 * channels), BF16),
            pltpu.VMEM((rows, channels), BF16),
            pltpu.VMEM((rows, channels), BF16),
            pltpu.VMEM((rows, 3 * channels), BF16),
            pltpu.VMEM((count, 16, width), BF16),
            pltpu.VMEM((count, 16, width), BF16),
            pltpu.VMEM((16, width), BF16),
            pltpu.VMEM((count, 16, width), BF16),
            dma((count,)),
            dma((count,)),
            dma((count,)),
            dma((count,)),
            dma((chunks,)),
            dma(()),
            dma(()),
            dma(()),
            dma(()),
        ],
        compiler_params=pltpu.CompilerParams(
            collective_id=0, has_side_effects=True, vmem_limit_bytes=56 * 1024 * 1024
        ),
    )(
        tokens.reshape(shape),
        cotangent.reshape(shape),
        norm1_gain.reshape(1, channels),
        w_qkv,
        w_out,
        bias,
        norm2_gain.reshape(1, channels),
        w_up,
        w_down,
        mask,
    )
    return (
        mixed.reshape(tokens.shape),
        grad_tokens.reshape(tokens.shape),
        sums[:, : 3 * channels] * factor,
        sums[:, 3 * channels :] * factor,
    )


def solution(mesh):
    placed = (P("gy", "gx", None), P("gy", "gx", None), P(), P(), P(), P(), P(), P(), P())
    return jax.shard_map(
        local,
        mesh=mesh,
        in_specs=placed,
        out_specs=(P("gy", "gx", None), P("gy", "gx", None), P(), P()),
        check_vma=False,
    )
```

```python
import functools
import math

import jax
import jax.numpy as jnp
from jax import lax
from jax.experimental import pallas as pl
from jax.experimental.pallas import tpu as pltpu
from jax.sharding import PartitionSpec as P

GRID = 8
MEMBERS = GRID * GRID
EPSILON = 1e-05
BATCH = 16
MESH = pl.DeviceIdType.MESH
F32 = jnp.float32
BF16 = jnp.bfloat16


def dot(a, b, da=1, db=0):
    return lax.dot_general(a, b, (((da,), (db,)), ((), ())), preferred_element_type=F32)


def unit_of(wide):
    centre = jnp.mean(wide, axis=-1, keepdims=True)
    shifted = wide - centre
    variance = jnp.mean(shifted * shifted, axis=-1, keepdims=True)
    inverse = lax.rsqrt(variance + EPSILON)
    return shifted * inverse, inverse


def chunk_work(block, result, weights, acc, work, heads):
    gain1, w_qkv, w_out, bias, gain2, w_up, w_down, mask = weights
    wide, xg, gg, normed, qkv, dctx, ctx, dqkv = work
    channels = xg.shape[-1]
    rows = BATCH * MEMBERS
    scale = 1.0 / math.sqrt(channels // heads)
    half = 128

    step = 256

    def regroup():
        for tensor, kept in ((0, xg), (1, gg)):
            value = block[tensor].astype(F32).reshape(rows, channels)
            for part in range(channels // half):
                wide[part] = value[:, part * half : (part + 1) * half]
            for group in range(BATCH):
                for part in range(channels // half):
                    kept[group * MEMBERS : (group + 1) * MEMBERS, part * half : (part + 1) * half] = wide[
                        part, pl.ds(group, MEMBERS, stride=BATCH), :
                    ].astype(BF16)

    def before(index, carry):
        at = pl.ds(pl.multiple_of(index * step, step), step)
        unit, inverse = unit_of(xg[at, :].astype(F32))
        low = (unit * gain1[...]).astype(BF16)
        normed[at, :] = low
        qkv[at, :] = dot(low, w_qkv[...]).astype(BF16)
        dctx[at, :] = dot(gg[at, :], w_out[...], 1, 1).astype(BF16)
        return carry

    def one_group(at):
        query = qkv[at, 0:channels]
        keys = qkv[at, channels : 2 * channels]
        values = qkv[at, 2 * channels : 3 * channels]
        spread = mask[...]
        query_wide = jnp.concatenate([query] * heads, axis=0) * spread
        d_wide = jnp.concatenate([dctx[at, :]] * heads, axis=0) * spread
        scores = dot(keys, query_wide, 1, 1) * scale + bias[...]
        top = jnp.max(scores, axis=0, keepdims=True)
        raised = jnp.exp(scores - top)
        probs = raised / jnp.sum(raised, axis=0, keepdims=True)
        low = probs.astype(BF16)
        d_probs = dot(values, d_wide, 1, 1)
        inner = jnp.sum(probs * d_probs, axis=0, keepdims=True)
        d_scaled = (probs * (d_probs - inner) * scale).astype(BF16)

        def gathered(left, right):
            full = dot(left, right, 0, 0)
            lane = lax.broadcasted_iota(jnp.int32, (MEMBERS, channels), 1) // (channels // heads)
            total = full[0:MEMBERS]
            for head in range(1, heads):
                total = jnp.where(lane == head, full[head * MEMBERS : (head + 1) * MEMBERS], total)
            return total

        ctx[at, :] = gathered(low, values).astype(BF16)
        dqkv[at, 0:channels] = gathered(d_scaled, keys).astype(BF16)
        dqkv[at, channels : 2 * channels] = dot(d_scaled, query_wide).astype(BF16)
        dqkv[at, 2 * channels : 3 * channels] = dot(low, d_wide).astype(BF16)

    def attend(index, carry):
        for inner in range(2):
            one_group(pl.ds(pl.multiple_of((2 * index + inner) * MEMBERS, MEMBERS), MEMBERS))
        return carry

    def attention():
        regroup()
        lax.fori_loop(0, rows // step, before, 0)
        lax.fori_loop(0, BATCH // 2, attend, 0)
        acc[:, 0 : 3 * channels] += dot(normed[...], dqkv[...], 0, 0)
        acc[:, 3 * channels : 4 * channels] += dot(ctx[...], gg[...], 0, 0)

    def spread_out(index, value):
        groups = step // MEMBERS
        for local in range(groups):
            for part in range(channels // half):
                wide[part, pl.ds(index * groups + local, MEMBERS, stride=BATCH), :] = value[
                    local * MEMBERS : (local + 1) * MEMBERS, part * half : (part + 1) * half
                ]

    def finish(tensor):
        value = jnp.concatenate([wide[part] for part in range(channels // half)], axis=1)
        result[tensor] = value.reshape(MEMBERS, BATCH, channels).astype(BF16)

    def forward(index, carry):
        at = pl.ds(pl.multiple_of(index * step, step), step)
        attended = (xg[at, :].astype(F32) + dot(ctx[at, :], w_out[...])).astype(BF16).astype(F32)
        unit, inverse = unit_of(attended)
        low = (unit * gain2[...]).astype(BF16)
        hidden = jax.nn.gelu(dot(low, w_up[...])).astype(BF16)
        spread_out(index, attended + dot(hidden, w_down[...]))
        return carry

    def backward(index, carry):
        at = pl.ds(pl.multiple_of(index * step, step), step)
        unit, inverse = unit_of(xg[at, :].astype(F32))
        d_unit = dot(dqkv[at, :], w_qkv[...], 1, 1) * gain1[...]
        d_x = inverse * (
            d_unit
            - jnp.mean(d_unit, axis=-1, keepdims=True)
            - unit * jnp.mean(d_unit * unit, axis=-1, keepdims=True)
        )
        spread_out(index, gg[at, :].astype(F32) + d_x)
        return carry

    def mlp():
        lax.fori_loop(0, rows // step, forward, 0)
        finish(0)

    def token_gradient():
        lax.fori_loop(0, rows // step, backward, 0)
        finish(1)

    return attention, mlp, token_gradient


def kernel(
    plan,
    tokens, cotangent, gain1, w_qkv, w_out, pos_bias, gain2, w_up, w_down,
    mixed, grad_tokens, grad_qkv, grad_out,
    inbox, outbox, acc, wide, xg, gg, normed, qkv, dctx, ctx, dqkv, bias, mask,
    parts, column_parts, column_sum, row_parts, share, row_shares, shares,
    sent_in, sent_out, sent_column, sent_row, sent_row_back, sent_column_back,
    chunk_sem, mixed_sem, grad_sem, sum_sem,
):
    row_devices, column_devices, row_part, extra, members, splits, strip, per_block, heads, factor = plan
    count = row_devices * column_devices
    gy = lax.axis_index("gy")
    gx = lax.axis_index("gx")
    me = gy * column_devices + gx

    def place(device):
        return device // column_devices, device % column_devices

    def home(device):
        row, column = place(device)
        return row * row_part + column // splits, (column % splits) * strip

    def seat(device):
        row, column = place(device)
        return (row // extra) * GRID + column * members, row % extra

    def peers(body):
        def step(index, carry):
            device = (me + index) % count
            body(index, device, place(device))
            return carry

        lax.fori_loop(1, count, step, 0)

    barrier = pltpu.get_barrier_semaphore()
    peers(lambda index, device, at: pl.semaphore_signal(barrier, inc=1, device_id=at, device_id_type=MESH))
    pl.semaphore_wait(barrier, count - 1)

    my_member, my_extra = seat(me)
    my_row, my_column = home(me)

    def send_block(piece, _):
        chunk = my_extra * per_block + piece
        span = pl.ds(my_member, members)

        def source(device, array):
            row, column = home(device)
            return array.at[row, :, pl.ds(pl.multiple_of(column + piece * BATCH, BATCH), BATCH), :]

        for tensor, array in ((0, tokens), (1, cotangent)):
            pltpu.make_async_copy(
                source(me, array), inbox.at[chunk, tensor, span], chunk_sem.at[chunk]
            ).start()

        def to_peer(index, device, at):
            for tensor, array in ((0, tokens), (1, cotangent)):
                pltpu.make_async_remote_copy(
                    src_ref=source(device, array),
                    dst_ref=inbox.at[chunk, tensor, span],
                    send_sem=sent_in.at[index],
                    recv_sem=chunk_sem.at[chunk],
                    device_id=at,
                    device_id_type=MESH,
                ).start()

        peers(to_peer)
        return _

    lax.fori_loop(0, per_block, send_block, 0)
    acc[...] = jnp.zeros_like(acc)
    bias[...] = pos_bias[...].T
    channels = mask.shape[1]
    mask[...] = (
        lax.broadcasted_iota(jnp.int32, mask.shape, 0) // MEMBERS
        == lax.broadcasted_iota(jnp.int32, mask.shape, 1) // (channels // heads)
    ).astype(F32).astype(BF16)
    weights = (gain1, w_qkv, w_out, bias, gain2, w_up, w_down, mask)
    work = (wide, xg, gg, normed, qkv, dctx, ctx, dqkv)
    targets = ((mixed, mixed_sem), (grad_tokens, grad_sem))

    def send_home(chunk, tensor):
        part = chunk // per_block
        piece = chunk % per_block
        column = pl.ds(pl.multiple_of(my_column + piece * BATCH, BATCH), BATCH)
        array, sem = targets[tensor]

        def keep():
            pltpu.make_async_copy(
                outbox.at[chunk, tensor, pl.ds(my_member, members)], array.at[my_row, :, column, :], sem
            ).start()

        def to_peer(index, device, at):
            member, its = seat(device)

            def send():
                pltpu.make_async_remote_copy(
                    src_ref=outbox.at[chunk, tensor, pl.ds(member, members)],
                    dst_ref=array.at[my_row, :, column, :],
                    send_sem=sent_out.at[index],
                    recv_sem=sem,
                    device_id=at,
                    device_id_type=MESH,
                ).start()

            if extra == 1:
                send()
            else:
                pl.when(its == part)(send)

        if extra == 1:
            keep()
        else:
            pl.when(my_extra == part)(keep)
        peers(to_peer)

    def exchange(stage, axis, source, target, sent):
        size, own = ((row_devices, gy), (column_devices, gx))[axis]
        pltpu.make_async_copy(source(own), target.at[own], sum_sem.at[stage]).start()

        def step(index, carry):
            other = (own + index) % size
            pltpu.make_async_remote_copy(
                src_ref=source(other),
                dst_ref=target.at[own],
                send_sem=sent.at[index],
                recv_sem=sum_sem.at[stage],
                device_id=((other, gx), (gy, other))[axis],
                device_id_type=MESH,
            ).start()
            return carry

        lax.fori_loop(1, size, step, 0)

    def arrive(stage, target):
        pltpu.make_async_copy(target, target, sum_sem.at[stage]).wait()

    height, width = share.shape
    across = acc.shape[1] // width

    def areas():
        for place_of in range(count):
            yield (
                place_of // row_devices,
                place_of % row_devices,
                place_of // across * height,
                place_of % across * width,
            )

    chunks = extra * per_block

    def one_chunk(chunk, _):
        pltpu.make_async_copy(inbox.at[chunk], inbox.at[chunk], chunk_sem.at[chunk]).wait()
        attention, mlp, token_gradient = chunk_work(
            inbox.at[chunk], outbox.at[chunk], weights, acc, work, heads
        )
        attention()

        @pl.when(chunk == chunks - 1)
        def begin_sums():
            for column, row, top, left in areas():
                parts[column, row] = acc[top : top + height, left : left + width].astype(BF16)
            exchange(0, 1, lambda other: parts.at[other], column_parts, sent_column)
            send_home(chunks - 2, 0)

        mlp()
        pl.when(chunk < chunks - 2)(lambda: send_home(chunk, 0))
        token_gradient()
        pl.when(chunk < chunks - 2)(lambda: send_home(chunk, 1))
        return _

    lax.fori_loop(0, chunks, one_chunk, 0)

    arrive(0, column_parts)
    column_sum[...] = jnp.sum(column_parts[...].astype(F32), axis=0).astype(BF16)
    exchange(1, 0, lambda other: column_sum.at[other], row_parts, sent_row)
    send_home(chunks - 2, 1)
    arrive(1, row_parts)
    share[...] = jnp.sum(row_parts[...].astype(F32), axis=0).astype(BF16)
    exchange(2, 0, lambda other: share, row_shares, sent_row_back)
    send_home(chunks - 1, 0)
    arrive(2, row_shares)
    exchange(3, 1, lambda other: row_shares, shares, sent_column_back)
    send_home(chunks - 1, 1)
    arrive(3, shares)
    for column, row, top, left in areas():
        value = shares[column, row].astype(F32) * factor
        cut = min(max(3 * channels - left, 0), width)
        if cut > 0:
            grad_qkv[top : top + height, left : left + cut] = value[:, :cut]
        if cut < width:
            start = left + cut - 3 * channels
            grad_out[top : top + height, start : start + width - cut] = value[:, cut:]

    def drain(index, device, at):
        moved = inbox.at[pl.ds(0, per_block), :, pl.ds(0, members)]
        pltpu.make_async_copy(moved, moved, sent_in.at[index]).wait()
        pltpu.make_async_copy(moved, moved, sent_out.at[index]).wait()

    peers(drain)
    for sent, size, moved in (
        (sent_column, column_devices, row_parts),
        (sent_row, row_devices, share),
        (sent_row_back, row_devices, share),
        (sent_column_back, column_devices, row_parts),
    ):
        for index in range(1, size):
            pltpu.make_async_copy(moved, moved, sent.at[index]).wait()
    pltpu.make_async_copy(mixed, mixed, mixed_sem).wait()
    pltpu.make_async_copy(grad_tokens, grad_tokens, grad_sem).wait()


def local(tokens, cotangent, norm1_gain, w_qkv, w_out, pos_bias, norm2_gain, w_up, w_down):
    tile_rows, tile_cols, channels = tokens.shape
    row_devices = lax.axis_size("gy")
    column_devices = lax.axis_size("gx")
    count = row_devices * column_devices
    heads, nodes = pos_bias.shape[:2]
    row_part = tile_rows // row_devices
    extra = row_devices // GRID
    members = GRID // column_devices
    stride = tile_cols // members
    splits = column_devices // row_part
    strip = stride // splits
    per_block = strip // BATCH
    chunks = extra * per_block
    factor = 1.0 / math.sqrt(tile_rows * tile_cols * count)
    plan = (row_devices, column_devices, row_part, extra, members, splits, strip, per_block, heads, factor)
    shape = (tile_rows, members, stride, channels)
    rows = BATCH * MEMBERS
    width = 4 * channels * channels // (16 * count)
    anywhere = pl.BlockSpec(memory_space=pl.ANY)
    vmem = pl.BlockSpec(memory_space=pltpu.VMEM)
    dma = pltpu.SemaphoreType.DMA
    box = (chunks, 2, MEMBERS, BATCH, channels)
    mixed, grad_tokens, grad_qkv, grad_out = pl.pallas_call(
        functools.partial(kernel, plan),
        out_shape=(
            jax.ShapeDtypeStruct(shape, BF16),
            jax.ShapeDtypeStruct(shape, BF16),
            jax.ShapeDtypeStruct((channels, 3 * channels), F32),
            jax.ShapeDtypeStruct((channels, channels), F32),
        ),
        in_specs=[anywhere, anywhere] + [vmem] * 7,
        out_specs=(anywhere, anywhere, vmem, vmem),
        scratch_shapes=[
            pltpu.VMEM(box, BF16),
            pltpu.VMEM(box, BF16),
            pltpu.VMEM((channels, 4 * channels), F32),
            pltpu.VMEM((channels // 128, rows, 128), F32),
            pltpu.VMEM((rows, channels), BF16),
            pltpu.VMEM((rows, channels), BF16),
            pltpu.VMEM((rows, channels), BF16),
            pltpu.VMEM((rows, 3 * channels), BF16),
            pltpu.VMEM((rows, channels), BF16),
            pltpu.VMEM((rows, channels), BF16),
            pltpu.VMEM((rows, 3 * channels), BF16),
            pltpu.VMEM((nodes, heads * nodes), F32),
            pltpu.VMEM((heads * nodes, channels), BF16),
            pltpu.VMEM((column_devices, row_devices, 16, width), BF16),
            pltpu.VMEM((column_devices, row_devices, 16, width), BF16),
            pltpu.VMEM((row_devices, 16, width), BF16),
            pltpu.VMEM((row_devices, 16, width), BF16),
            pltpu.VMEM((16, width), BF16),
            pltpu.VMEM((row_devices, 16, width), BF16),
            pltpu.VMEM((column_devices, row_devices, 16, width), BF16),
            dma((count,)),
            dma((count,)),
            dma((column_devices,)),
            dma((row_devices,)),
            dma((row_devices,)),
            dma((column_devices,)),
            dma((chunks,)),
            dma(()),
            dma(()),
            dma((4,)),
        ],
        compiler_params=pltpu.CompilerParams(
            collective_id=0, has_side_effects=True, vmem_limit_bytes=56 * 1024 * 1024
        ),
    )(
        tokens.reshape(shape),
        cotangent.reshape(shape),
        norm1_gain.reshape(1, channels),
        w_qkv,
        w_out,
        pos_bias.reshape(heads * nodes, nodes),
        norm2_gain.reshape(1, channels),
        w_up,
        w_down,
    )
    return (
        mixed.reshape(tokens.shape),
        grad_tokens.reshape(tokens.shape),
        grad_qkv,
        grad_out,
    )


def solution(mesh):
    placed = (P("gy", "gx", None), P("gy", "gx", None), P(), P(), P(), P(), P(), P(), P())
    return jax.shard_map(
        local,
        mesh=mesh,
        in_specs=placed,
        out_specs=(P("gy", "gx", None), P("gy", "gx", None), P(), P()),
        check_vma=False,
    )
```

```python
import functools
import math

import jax
import jax.numpy as jnp
from jax import lax
from jax.experimental import pallas as pl
from jax.experimental.pallas import tpu as pltpu
from jax.sharding import PartitionSpec as P

GRID = 8
MEMBERS = GRID * GRID
EPSILON = 1e-05
BATCH = 16
STRIDE = 13
MESH = pl.DeviceIdType.MESH
F32 = jnp.float32
BF16 = jnp.bfloat16


def dot(a, b, da=1, db=0):
    return lax.dot_general(a, b, (((da,), (db,)), ((), ())), preferred_element_type=F32)


def unit_of(wide):
    centre = jnp.mean(wide, axis=-1, keepdims=True)
    shifted = wide - centre
    variance = jnp.mean(shifted * shifted, axis=-1, keepdims=True)
    inverse = lax.rsqrt(variance + EPSILON)
    return shifted * inverse, inverse


def chunk_work(block, result, weights, acc, work, heads):
    gain1, w_qkv, w_out, bias, gain2, w_up, w_down, mask = weights
    wide, xg, gg, normed, qkv, dctx, ctx, dqkv = work
    channels = xg.shape[-1]
    rows = BATCH * MEMBERS
    scale = 1.0 / math.sqrt(channels // heads)
    half = 128

    step = 256

    def regroup():
        for tensor, kept in ((0, xg), (1, gg)):
            value = block[tensor].astype(F32).reshape(rows, channels)
            for part in range(channels // half):
                wide[part] = value[:, part * half : (part + 1) * half]
            for group in range(BATCH):
                for part in range(channels // half):
                    kept[group * MEMBERS : (group + 1) * MEMBERS, part * half : (part + 1) * half] = wide[
                        part, pl.ds(group, MEMBERS, stride=BATCH), :
                    ].astype(BF16)

    def before(index, carry):
        at = pl.ds(pl.multiple_of(index * step, step), step)
        unit, inverse = unit_of(xg[at, :].astype(F32))
        low = (unit * gain1[...]).astype(BF16)
        normed[at, :] = low
        qkv[at, :] = dot(low, w_qkv[...]).astype(BF16)
        dctx[at, :] = dot(gg[at, :], w_out[...], 1, 1).astype(BF16)
        return carry

    def one_group(at):
        query = qkv[at, 0:channels]
        keys = qkv[at, channels : 2 * channels]
        values = qkv[at, 2 * channels : 3 * channels]
        spread = mask[...]
        query_wide = jnp.concatenate([query] * heads, axis=0) * spread
        d_wide = jnp.concatenate([dctx[at, :]] * heads, axis=0) * spread
        scores = dot(keys, query_wide, 1, 1) * scale + bias[...]
        top = jnp.max(scores, axis=0, keepdims=True)
        raised = jnp.exp(scores - top)
        probs = raised / jnp.sum(raised, axis=0, keepdims=True)
        low = probs.astype(BF16)
        d_probs = dot(values, d_wide, 1, 1)
        inner = jnp.sum(probs * d_probs, axis=0, keepdims=True)
        d_scaled = (probs * (d_probs - inner) * scale).astype(BF16)

        def gathered(left, right):
            full = dot(left, right, 0, 0)
            lane = lax.broadcasted_iota(jnp.int32, (MEMBERS, channels), 1) // (channels // heads)
            total = full[0:MEMBERS]
            for head in range(1, heads):
                total = jnp.where(lane == head, full[head * MEMBERS : (head + 1) * MEMBERS], total)
            return total

        ctx[at, :] = gathered(low, values).astype(BF16)
        dqkv[at, 0:channels] = gathered(d_scaled, keys).astype(BF16)
        dqkv[at, channels : 2 * channels] = dot(d_scaled, query_wide).astype(BF16)
        dqkv[at, 2 * channels : 3 * channels] = dot(low, d_wide).astype(BF16)

    def attend(index, carry):
        for inner in range(2):
            one_group(pl.ds(pl.multiple_of((2 * index + inner) * MEMBERS, MEMBERS), MEMBERS))
        return carry

    def attention():
        regroup()
        lax.fori_loop(0, rows // step, before, 0)
        lax.fori_loop(0, BATCH // 2, attend, 0)
        acc[:, 0 : 3 * channels] += dot(normed[...], dqkv[...], 0, 0)
        acc[:, 3 * channels : 4 * channels] += dot(ctx[...], gg[...], 0, 0)

    def spread_out(index, value):
        groups = step // MEMBERS
        for local in range(groups):
            for part in range(channels // half):
                wide[part, pl.ds(index * groups + local, MEMBERS, stride=BATCH), :] = value[
                    local * MEMBERS : (local + 1) * MEMBERS, part * half : (part + 1) * half
                ]

    def finish(tensor):
        value = jnp.concatenate([wide[part] for part in range(channels // half)], axis=1)
        result[tensor] = value.reshape(MEMBERS, BATCH, channels).astype(BF16)

    def forward(index, carry):
        at = pl.ds(pl.multiple_of(index * step, step), step)
        attended = (xg[at, :].astype(F32) + dot(ctx[at, :], w_out[...])).astype(BF16).astype(F32)
        unit, inverse = unit_of(attended)
        low = (unit * gain2[...]).astype(BF16)
        hidden = jax.nn.gelu(dot(low, w_up[...])).astype(BF16)
        spread_out(index, attended + dot(hidden, w_down[...]))
        return carry

    def backward(index, carry):
        at = pl.ds(pl.multiple_of(index * step, step), step)
        unit, inverse = unit_of(xg[at, :].astype(F32))
        d_unit = dot(dqkv[at, :], w_qkv[...], 1, 1) * gain1[...]
        d_x = inverse * (
            d_unit
            - jnp.mean(d_unit, axis=-1, keepdims=True)
            - unit * jnp.mean(d_unit * unit, axis=-1, keepdims=True)
        )
        spread_out(index, gg[at, :].astype(F32) + d_x)
        return carry

    def mlp():
        lax.fori_loop(0, rows // step, forward, 0)
        finish(0)

    def token_gradient():
        lax.fori_loop(0, rows // step, backward, 0)
        finish(1)

    return attention, mlp, token_gradient


def kernel(
    plan,
    tokens, cotangent, gain1, w_qkv, w_out, pos_bias, gain2, w_up, w_down,
    mixed, grad_tokens, grad_qkv, grad_out,
    inbox, outbox, acc, wide, xg, gg, normed, qkv, dctx, ctx, dqkv, bias, mask,
    parts, column_parts, column_sum, row_parts, share, row_shares, shares,
    sent_in, sent_out, sent_column, sent_row, sent_row_back, sent_column_back,
    chunk_sem, mixed_sem, grad_sem, sum_sem,
):
    row_devices, column_devices, row_part, extra, members, splits, strip, per_block, heads, factor = plan
    count = row_devices * column_devices
    gy = lax.axis_index("gy")
    gx = lax.axis_index("gx")
    me = gy * column_devices + gx

    def place(device):
        return device // column_devices, device % column_devices

    def home(device):
        row, column = place(device)
        return row * row_part + column // splits, (column % splits) * strip

    def seat(device):
        row, column = place(device)
        return (row // extra) * GRID + column * members, row % extra

    def peers(body):
        def step(index, carry):
            device = (me + index * STRIDE) % count
            body(index, device, place(device))
            return carry

        lax.fori_loop(1, count, step, 0)

    barrier = pltpu.get_barrier_semaphore()
    peers(lambda index, device, at: pl.semaphore_signal(barrier, inc=1, device_id=at, device_id_type=MESH))
    pl.semaphore_wait(barrier, count - 1)

    my_member, my_extra = seat(me)
    my_row, my_column = home(me)

    def send_block(piece, _):
        chunk = my_extra * per_block + piece
        span = pl.ds(my_member, members)

        def source(device, array):
            row, column = home(device)
            return array.at[row, :, pl.ds(pl.multiple_of(column + piece * BATCH, BATCH), BATCH), :]

        for tensor, array in ((0, tokens), (1, cotangent)):
            pltpu.make_async_copy(
                source(me, array), inbox.at[chunk, tensor, span], chunk_sem.at[chunk]
            ).start()

        def to_peer(index, device, at):
            for tensor, array in ((0, tokens), (1, cotangent)):
                pltpu.make_async_remote_copy(
                    src_ref=source(device, array),
                    dst_ref=inbox.at[chunk, tensor, span],
                    send_sem=sent_in.at[index],
                    recv_sem=chunk_sem.at[chunk],
                    device_id=at,
                    device_id_type=MESH,
                ).start()

        peers(to_peer)
        return _

    lax.fori_loop(0, per_block, send_block, 0)
    acc[...] = jnp.zeros_like(acc)
    bias[...] = pos_bias[...].T
    channels = mask.shape[1]
    mask[...] = (
        lax.broadcasted_iota(jnp.int32, mask.shape, 0) // MEMBERS
        == lax.broadcasted_iota(jnp.int32, mask.shape, 1) // (channels // heads)
    ).astype(F32).astype(BF16)
    weights = (gain1, w_qkv, w_out, bias, gain2, w_up, w_down, mask)
    work = (wide, xg, gg, normed, qkv, dctx, ctx, dqkv)
    targets = ((mixed, mixed_sem), (grad_tokens, grad_sem))

    def send_home(chunk, tensor):
        part = chunk // per_block
        piece = chunk % per_block
        column = pl.ds(pl.multiple_of(my_column + piece * BATCH, BATCH), BATCH)
        array, sem = targets[tensor]

        def keep():
            pltpu.make_async_copy(
                outbox.at[chunk, tensor, pl.ds(my_member, members)], array.at[my_row, :, column, :], sem
            ).start()

        def to_peer(index, device, at):
            member, its = seat(device)

            def send():
                pltpu.make_async_remote_copy(
                    src_ref=outbox.at[chunk, tensor, pl.ds(member, members)],
                    dst_ref=array.at[my_row, :, column, :],
                    send_sem=sent_out.at[index],
                    recv_sem=sem,
                    device_id=at,
                    device_id_type=MESH,
                ).start()

            if extra == 1:
                send()
            else:
                pl.when(its == part)(send)

        if extra == 1:
            keep()
        else:
            pl.when(my_extra == part)(keep)
        peers(to_peer)

    def exchange(stage, axis, source, target, sent):
        size, own = ((row_devices, gy), (column_devices, gx))[axis]
        pltpu.make_async_copy(source(own), target.at[own], sum_sem.at[stage]).start()

        def step(index, carry):
            other = (own + index) % size
            pltpu.make_async_remote_copy(
                src_ref=source(other),
                dst_ref=target.at[own],
                send_sem=sent.at[index],
                recv_sem=sum_sem.at[stage],
                device_id=((other, gx), (gy, other))[axis],
                device_id_type=MESH,
            ).start()
            return carry

        lax.fori_loop(1, size, step, 0)

    def arrive(stage, target):
        pltpu.make_async_copy(target, target, sum_sem.at[stage]).wait()

    height, width = share.shape
    across = acc.shape[1] // width

    def areas():
        for place_of in range(count):
            yield (
                place_of // row_devices,
                place_of % row_devices,
                place_of // across * height,
                place_of % across * width,
            )

    chunks = extra * per_block

    def one_chunk(chunk, _):
        pltpu.make_async_copy(inbox.at[chunk], inbox.at[chunk], chunk_sem.at[chunk]).wait()
        attention, mlp, token_gradient = chunk_work(
            inbox.at[chunk], outbox.at[chunk], weights, acc, work, heads
        )
        attention()

        @pl.when(chunk == chunks - 1)
        def begin_sums():
            for column, row, top, left in areas():
                parts[column, row] = acc[top : top + height, left : left + width].astype(BF16)
            exchange(0, 1, lambda other: parts.at[other], column_parts, sent_column)
            send_home(chunks - 2, 0)

        mlp()
        pl.when(chunk < chunks - 2)(lambda: send_home(chunk, 0))
        token_gradient()
        pl.when(chunk < chunks - 2)(lambda: send_home(chunk, 1))
        return _

    lax.fori_loop(0, chunks, one_chunk, 0)

    arrive(0, column_parts)
    column_sum[...] = jnp.sum(column_parts[...].astype(F32), axis=0).astype(BF16)
    exchange(1, 0, lambda other: column_sum.at[other], row_parts, sent_row)
    send_home(chunks - 2, 1)
    arrive(1, row_parts)
    share[...] = jnp.sum(row_parts[...].astype(F32), axis=0).astype(BF16)
    exchange(2, 0, lambda other: share, row_shares, sent_row_back)
    send_home(chunks - 1, 0)
    arrive(2, row_shares)
    exchange(3, 1, lambda other: row_shares, shares, sent_column_back)
    send_home(chunks - 1, 1)
    arrive(3, shares)
    for column, row, top, left in areas():
        value = shares[column, row].astype(F32) * factor
        cut = min(max(3 * channels - left, 0), width)
        if cut > 0:
            grad_qkv[top : top + height, left : left + cut] = value[:, :cut]
        if cut < width:
            start = left + cut - 3 * channels
            grad_out[top : top + height, start : start + width - cut] = value[:, cut:]

    def drain(index, device, at):
        moved = inbox.at[pl.ds(0, per_block), :, pl.ds(0, members)]
        pltpu.make_async_copy(moved, moved, sent_in.at[index]).wait()
        pltpu.make_async_copy(moved, moved, sent_out.at[index]).wait()

    peers(drain)
    for sent, size, moved in (
        (sent_column, column_devices, row_parts),
        (sent_row, row_devices, share),
        (sent_row_back, row_devices, share),
        (sent_column_back, column_devices, row_parts),
    ):
        for index in range(1, size):
            pltpu.make_async_copy(moved, moved, sent.at[index]).wait()
    pltpu.make_async_copy(mixed, mixed, mixed_sem).wait()
    pltpu.make_async_copy(grad_tokens, grad_tokens, grad_sem).wait()


def local(tokens, cotangent, norm1_gain, w_qkv, w_out, pos_bias, norm2_gain, w_up, w_down):
    tile_rows, tile_cols, channels = tokens.shape
    row_devices = lax.axis_size("gy")
    column_devices = lax.axis_size("gx")
    count = row_devices * column_devices
    heads, nodes = pos_bias.shape[:2]
    row_part = tile_rows // row_devices
    extra = row_devices // GRID
    members = GRID // column_devices
    stride = tile_cols // members
    splits = column_devices // row_part
    strip = stride // splits
    per_block = strip // BATCH
    chunks = extra * per_block
    factor = 1.0 / math.sqrt(tile_rows * tile_cols * count)
    plan = (row_devices, column_devices, row_part, extra, members, splits, strip, per_block, heads, factor)
    shape = (tile_rows, members, stride, channels)
    rows = BATCH * MEMBERS
    width = 4 * channels * channels // (16 * count)
    anywhere = pl.BlockSpec(memory_space=pl.ANY)
    vmem = pl.BlockSpec(memory_space=pltpu.VMEM)
    dma = pltpu.SemaphoreType.DMA
    box = (chunks, 2, MEMBERS, BATCH, channels)
    mixed, grad_tokens, grad_qkv, grad_out = pl.pallas_call(
        functools.partial(kernel, plan),
        out_shape=(
            jax.ShapeDtypeStruct(shape, BF16),
            jax.ShapeDtypeStruct(shape, BF16),
            jax.ShapeDtypeStruct((channels, 3 * channels), F32),
            jax.ShapeDtypeStruct((channels, channels), F32),
        ),
        in_specs=[anywhere, anywhere] + [vmem] * 7,
        out_specs=(anywhere, anywhere, vmem, vmem),
        scratch_shapes=[
            pltpu.VMEM(box, BF16),
            pltpu.VMEM(box, BF16),
            pltpu.VMEM((channels, 4 * channels), F32),
            pltpu.VMEM((channels // 128, rows, 128), F32),
            pltpu.VMEM((rows, channels), BF16),
            pltpu.VMEM((rows, channels), BF16),
            pltpu.VMEM((rows, channels), BF16),
            pltpu.VMEM((rows, 3 * channels), BF16),
            pltpu.VMEM((rows, channels), BF16),
            pltpu.VMEM((rows, channels), BF16),
            pltpu.VMEM((rows, 3 * channels), BF16),
            pltpu.VMEM((nodes, heads * nodes), F32),
            pltpu.VMEM((heads * nodes, channels), BF16),
            pltpu.VMEM((column_devices, row_devices, 16, width), BF16),
            pltpu.VMEM((column_devices, row_devices, 16, width), BF16),
            pltpu.VMEM((row_devices, 16, width), BF16),
            pltpu.VMEM((row_devices, 16, width), BF16),
            pltpu.VMEM((16, width), BF16),
            pltpu.VMEM((row_devices, 16, width), BF16),
            pltpu.VMEM((column_devices, row_devices, 16, width), BF16),
            dma((count,)),
            dma((count,)),
            dma((column_devices,)),
            dma((row_devices,)),
            dma((row_devices,)),
            dma((column_devices,)),
            dma((chunks,)),
            dma(()),
            dma(()),
            dma((4,)),
        ],
        compiler_params=pltpu.CompilerParams(
            collective_id=0, has_side_effects=True, vmem_limit_bytes=56 * 1024 * 1024
        ),
    )(
        tokens.reshape(shape),
        cotangent.reshape(shape),
        norm1_gain.reshape(1, channels),
        w_qkv,
        w_out,
        pos_bias.reshape(heads * nodes, nodes),
        norm2_gain.reshape(1, channels),
        w_up,
        w_down,
    )
    return (
        mixed.reshape(tokens.shape),
        grad_tokens.reshape(tokens.shape),
        grad_qkv,
        grad_out,
    )


def solution(mesh):
    placed = (P("gy", "gx", None), P("gy", "gx", None), P(), P(), P(), P(), P(), P(), P())
    return jax.shard_map(
        local,
        mesh=mesh,
        in_specs=placed,
        out_specs=(P("gy", "gx", None), P("gy", "gx", None), P(), P()),
        check_vma=False,
    )
```

```python
import functools
import math

import jax
import jax.numpy as jnp
from jax import lax
from jax.experimental import pallas as pl
from jax.experimental.pallas import tpu as pltpu
from jax.sharding import PartitionSpec as P

GRID = 8
MEMBERS = GRID * GRID
EPSILON = 1e-05
BATCH = 16
MESH = pl.DeviceIdType.MESH
F32 = jnp.float32
BF16 = jnp.bfloat16


def dot(a, b, da=1, db=0):
    return lax.dot_general(a, b, (((da,), (db,)), ((), ())), preferred_element_type=F32)


def unit_of(wide):
    centre = jnp.mean(wide, axis=-1, keepdims=True)
    shifted = wide - centre
    variance = jnp.mean(shifted * shifted, axis=-1, keepdims=True)
    inverse = lax.rsqrt(variance + EPSILON)
    return shifted * inverse, inverse


def chunk_work(block, result, weights, acc, work, heads):
    gain1, w_qkv, w_out, bias, gain2, w_up, w_down, mask = weights
    wide, xg, gg, normed, qkv, dctx, ctx, dqkv = work
    channels = xg.shape[-1]
    rows = BATCH * MEMBERS
    scale = 1.0 / math.sqrt(channels // heads)
    half = 128

    step = 256

    def regroup():
        for tensor, kept in ((0, xg), (1, gg)):
            value = block[tensor].astype(F32).reshape(rows, channels)
            for part in range(channels // half):
                wide[part] = value[:, part * half : (part + 1) * half]
            for group in range(BATCH):
                for part in range(channels // half):
                    kept[group * MEMBERS : (group + 1) * MEMBERS, part * half : (part + 1) * half] = wide[
                        part, pl.ds(group, MEMBERS, stride=BATCH), :
                    ].astype(BF16)

    def before(index, carry):
        at = pl.ds(pl.multiple_of(index * step, step), step)
        unit, inverse = unit_of(xg[at, :].astype(F32))
        low = (unit * gain1[...]).astype(BF16)
        normed[at, :] = low
        qkv[at, :] = dot(low, w_qkv[...]).astype(BF16)
        dctx[at, :] = dot(gg[at, :], w_out[...], 1, 1).astype(BF16)
        return carry

    lanes = 128
    head_width = channels // heads
    span_heads = lanes // head_width
    span = span_heads * MEMBERS

    def some_heads(at, which):
        first = which * lanes
        query = qkv[at, first : first + lanes]
        keys = qkv[at, channels + first : channels + first + lanes]
        values = qkv[at, 2 * channels + first : 2 * channels + first + lanes]
        spread = mask[...]
        query_wide = jnp.concatenate([query] * span_heads, axis=0) * spread
        d_wide = jnp.concatenate([dctx[at, first : first + lanes]] * span_heads, axis=0) * spread
        scores = dot(keys, query_wide, 1, 1) * scale + bias[:, which * span : (which + 1) * span]
        top = jnp.max(scores, axis=0, keepdims=True)
        raised = jnp.exp(scores - top)
        probs = raised / jnp.sum(raised, axis=0, keepdims=True)
        low = probs.astype(BF16)
        d_probs = dot(values, d_wide, 1, 1)
        inner = jnp.sum(probs * d_probs, axis=0, keepdims=True)
        d_scaled = (probs * (d_probs - inner) * scale).astype(BF16)

        def gathered(left, right):
            full = dot(left, right, 0, 0)
            lane = lax.broadcasted_iota(jnp.int32, (MEMBERS, lanes), 1) // head_width
            total = full[0:MEMBERS]
            for head in range(1, span_heads):
                total = jnp.where(lane == head, full[head * MEMBERS : (head + 1) * MEMBERS], total)
            return total

        ctx[at, first : first + lanes] = gathered(low, values).astype(BF16)
        dqkv[at, first : first + lanes] = gathered(d_scaled, keys).astype(BF16)
        dqkv[at, channels + first : channels + first + lanes] = dot(d_scaled, query_wide).astype(BF16)
        dqkv[at, 2 * channels + first : 2 * channels + first + lanes] = dot(low, d_wide).astype(BF16)

    together = 4

    def attend(index, carry):
        for inner in range(together):
            at = pl.ds(pl.multiple_of((together * index + inner) * MEMBERS, MEMBERS), MEMBERS)
            for which in range(channels // lanes):
                some_heads(at, which)
        return carry

    def attention():
        regroup()
        lax.fori_loop(0, rows // step, before, 0)
        lax.fori_loop(0, BATCH // together, attend, 0)
        acc[:, 0 : 3 * channels] += dot(normed[...], dqkv[...], 0, 0)
        acc[:, 3 * channels : 4 * channels] += dot(ctx[...], gg[...], 0, 0)

    def spread_out(index, value):
        groups = step // MEMBERS
        for local in range(groups):
            for part in range(channels // half):
                wide[part, pl.ds(index * groups + local, MEMBERS, stride=BATCH), :] = value[
                    local * MEMBERS : (local + 1) * MEMBERS, part * half : (part + 1) * half
                ]

    def finish(tensor):
        value = jnp.concatenate([wide[part] for part in range(channels // half)], axis=1)
        result[tensor] = value.reshape(MEMBERS, BATCH, channels).astype(BF16)

    def forward(index, carry):
        at = pl.ds(pl.multiple_of(index * step, step), step)
        attended = (xg[at, :].astype(F32) + dot(ctx[at, :], w_out[...])).astype(BF16).astype(F32)
        unit, inverse = unit_of(attended)
        low = (unit * gain2[...]).astype(BF16)
        hidden = jax.nn.gelu(dot(low, w_up[...])).astype(BF16)
        spread_out(index, attended + dot(hidden, w_down[...]))
        return carry

    def backward(index, carry):
        at = pl.ds(pl.multiple_of(index * step, step), step)
        unit, inverse = unit_of(xg[at, :].astype(F32))
        d_unit = dot(dqkv[at, :], w_qkv[...], 1, 1) * gain1[...]
        d_x = inverse * (
            d_unit
            - jnp.mean(d_unit, axis=-1, keepdims=True)
            - unit * jnp.mean(d_unit * unit, axis=-1, keepdims=True)
        )
        spread_out(index, gg[at, :].astype(F32) + d_x)
        return carry

    def mlp():
        lax.fori_loop(0, rows // step, forward, 0)
        finish(0)

    def token_gradient():
        lax.fori_loop(0, rows // step, backward, 0)
        finish(1)

    return attention, mlp, token_gradient


def kernel(
    plan,
    tokens, cotangent, gain1, w_qkv, w_out, pos_bias, gain2, w_up, w_down,
    mixed, grad_tokens, grad_qkv, grad_out,
    inbox, outbox, acc, wide, xg, gg, normed, qkv, dctx, ctx, dqkv, bias, mask,
    parts, column_parts, column_sum, row_parts, share, row_shares, shares,
    sent_in, sent_out, sent_column, sent_row, sent_row_back, sent_column_back,
    chunk_sem, mixed_sem, grad_sem, sum_sem,
):
    row_devices, column_devices, row_part, extra, members, splits, strip, per_block, heads, factor = plan
    count = row_devices * column_devices
    gy = lax.axis_index("gy")
    gx = lax.axis_index("gx")
    me = gy * column_devices + gx

    def place(device):
        return device // column_devices, device % column_devices

    def home(device):
        row, column = place(device)
        return row * row_part + column // splits, (column % splits) * strip

    def seat(device):
        row, column = place(device)
        return (row // extra) * GRID + column * members, row % extra

    def peers(body):
        def step(index, carry):
            device = (me + index) % count
            body(index, device, place(device))
            return carry

        lax.fori_loop(1, count, step, 0)

    barrier = pltpu.get_barrier_semaphore()
    peers(lambda index, device, at: pl.semaphore_signal(barrier, inc=1, device_id=at, device_id_type=MESH))
    pl.semaphore_wait(barrier, count - 1)

    my_member, my_extra = seat(me)
    my_row, my_column = home(me)

    def send_block(piece, _):
        chunk = my_extra * per_block + piece
        span = pl.ds(my_member, members)

        def source(device, array):
            row, column = home(device)
            return array.at[row, :, pl.ds(pl.multiple_of(column + piece * BATCH, BATCH), BATCH), :]

        for tensor, array in ((0, tokens), (1, cotangent)):
            pltpu.make_async_copy(
                source(me, array), inbox.at[chunk, tensor, span], chunk_sem.at[chunk]
            ).start()

        def to_peer(index, device, at):
            for tensor, array in ((0, tokens), (1, cotangent)):
                pltpu.make_async_remote_copy(
                    src_ref=source(device, array),
                    dst_ref=inbox.at[chunk, tensor, span],
                    send_sem=sent_in.at[index],
                    recv_sem=chunk_sem.at[chunk],
                    device_id=at,
                    device_id_type=MESH,
                ).start()

        peers(to_peer)
        return _

    lax.fori_loop(0, per_block, send_block, 0)
    acc[...] = jnp.zeros_like(acc)
    bias[...] = pos_bias[...].T
    channels = acc.shape[0]
    mask[...] = (
        lax.broadcasted_iota(jnp.int32, mask.shape, 0) // MEMBERS
        == lax.broadcasted_iota(jnp.int32, mask.shape, 1) // (channels // heads)
    ).astype(F32).astype(BF16)
    weights = (gain1, w_qkv, w_out, bias, gain2, w_up, w_down, mask)
    work = (wide, xg, gg, normed, qkv, dctx, ctx, dqkv)
    targets = ((mixed, mixed_sem), (grad_tokens, grad_sem))

    def send_home(chunk, tensor):
        part = chunk // per_block
        piece = chunk % per_block
        column = pl.ds(pl.multiple_of(my_column + piece * BATCH, BATCH), BATCH)
        array, sem = targets[tensor]

        def keep():
            pltpu.make_async_copy(
                outbox.at[chunk, tensor, pl.ds(my_member, members)], array.at[my_row, :, column, :], sem
            ).start()

        def to_peer(index, device, at):
            member, its = seat(device)

            def send():
                pltpu.make_async_remote_copy(
                    src_ref=outbox.at[chunk, tensor, pl.ds(member, members)],
                    dst_ref=array.at[my_row, :, column, :],
                    send_sem=sent_out.at[index],
                    recv_sem=sem,
                    device_id=at,
                    device_id_type=MESH,
                ).start()

            if extra == 1:
                send()
            else:
                pl.when(its == part)(send)

        if extra == 1:
            keep()
        else:
            pl.when(my_extra == part)(keep)
        peers(to_peer)

    def exchange(stage, axis, source, target, sent):
        size, own = ((row_devices, gy), (column_devices, gx))[axis]
        pltpu.make_async_copy(source(own), target.at[own], sum_sem.at[stage]).start()

        def step(index, carry):
            other = (own + index) % size
            pltpu.make_async_remote_copy(
                src_ref=source(other),
                dst_ref=target.at[own],
                send_sem=sent.at[index],
                recv_sem=sum_sem.at[stage],
                device_id=((other, gx), (gy, other))[axis],
                device_id_type=MESH,
            ).start()
            return carry

        lax.fori_loop(1, size, step, 0)

    def arrive(stage, target):
        pltpu.make_async_copy(target, target, sum_sem.at[stage]).wait()

    height, width = share.shape
    across = acc.shape[1] // width

    def areas():
        for place_of in range(count):
            yield (
                place_of // row_devices,
                place_of % row_devices,
                place_of // across * height,
                place_of % across * width,
            )

    chunks = extra * per_block

    def one_chunk(chunk, _):
        pltpu.make_async_copy(inbox.at[chunk], inbox.at[chunk], chunk_sem.at[chunk]).wait()
        attention, mlp, token_gradient = chunk_work(
            inbox.at[chunk], outbox.at[chunk], weights, acc, work, heads
        )
        attention()

        @pl.when(chunk == chunks - 1)
        def begin_sums():
            for column, row, top, left in areas():
                parts[column, row] = acc[top : top + height, left : left + width].astype(BF16)
            exchange(0, 1, lambda other: parts.at[other], column_parts, sent_column)
            send_home(chunks - 2, 1)

        mlp()
        send_home(chunk, 0)
        token_gradient()
        pl.when(chunk < chunks - 2)(lambda: send_home(chunk, 1))
        return _

    lax.fori_loop(0, chunks, one_chunk, 0)

    arrive(0, column_parts)
    column_sum[...] = jnp.sum(column_parts[...].astype(F32), axis=0).astype(BF16)
    exchange(1, 0, lambda other: column_sum.at[other], row_parts, sent_row)
    arrive(1, row_parts)
    share[...] = jnp.sum(row_parts[...].astype(F32), axis=0).astype(BF16)
    exchange(2, 0, lambda other: share, row_shares, sent_row_back)
    send_home(chunks - 1, 1)
    arrive(2, row_shares)
    exchange(3, 1, lambda other: row_shares, shares, sent_column_back)
    arrive(3, shares)
    for column, row, top, left in areas():
        value = shares[column, row].astype(F32) * factor
        cut = min(max(3 * channels - left, 0), width)
        if cut > 0:
            grad_qkv[top : top + height, left : left + cut] = value[:, :cut]
        if cut < width:
            start = left + cut - 3 * channels
            grad_out[top : top + height, start : start + width - cut] = value[:, cut:]

    def drain(index, device, at):
        moved = inbox.at[pl.ds(0, per_block), :, pl.ds(0, members)]
        pltpu.make_async_copy(moved, moved, sent_in.at[index]).wait()
        pltpu.make_async_copy(moved, moved, sent_out.at[index]).wait()

    peers(drain)
    for sent, size, moved in (
        (sent_column, column_devices, row_parts),
        (sent_row, row_devices, share),
        (sent_row_back, row_devices, share),
        (sent_column_back, column_devices, row_parts),
    ):
        for index in range(1, size):
            pltpu.make_async_copy(moved, moved, sent.at[index]).wait()
    pltpu.make_async_copy(mixed, mixed, mixed_sem).wait()
    pltpu.make_async_copy(grad_tokens, grad_tokens, grad_sem).wait()


def local(tokens, cotangent, norm1_gain, w_qkv, w_out, pos_bias, norm2_gain, w_up, w_down):
    tile_rows, tile_cols, channels = tokens.shape
    row_devices = lax.axis_size("gy")
    column_devices = lax.axis_size("gx")
    count = row_devices * column_devices
    heads, nodes = pos_bias.shape[:2]
    row_part = tile_rows // row_devices
    extra = row_devices // GRID
    members = GRID // column_devices
    stride = tile_cols // members
    splits = column_devices // row_part
    strip = stride // splits
    per_block = strip // BATCH
    chunks = extra * per_block
    factor = 1.0 / math.sqrt(tile_rows * tile_cols * count)
    plan = (row_devices, column_devices, row_part, extra, members, splits, strip, per_block, heads, factor)
    shape = (tile_rows, members, stride, channels)
    rows = BATCH * MEMBERS
    width = 4 * channels * channels // (16 * count)
    anywhere = pl.BlockSpec(memory_space=pl.ANY)
    vmem = pl.BlockSpec(memory_space=pltpu.VMEM)
    dma = pltpu.SemaphoreType.DMA
    box = (chunks, 2, MEMBERS, BATCH, channels)
    mixed, grad_tokens, grad_qkv, grad_out = pl.pallas_call(
        functools.partial(kernel, plan),
        out_shape=(
            jax.ShapeDtypeStruct(shape, BF16),
            jax.ShapeDtypeStruct(shape, BF16),
            jax.ShapeDtypeStruct((channels, 3 * channels), F32),
            jax.ShapeDtypeStruct((channels, channels), F32),
        ),
        in_specs=[anywhere, anywhere] + [vmem] * 7,
        out_specs=(anywhere, anywhere, vmem, vmem),
        scratch_shapes=[
            pltpu.VMEM(box, BF16),
            pltpu.VMEM(box, BF16),
            pltpu.VMEM((channels, 4 * channels), F32),
            pltpu.VMEM((channels // 128, rows, 128), F32),
            pltpu.VMEM((rows, channels), BF16),
            pltpu.VMEM((rows, channels), BF16),
            pltpu.VMEM((rows, channels), BF16),
            pltpu.VMEM((rows, 3 * channels), BF16),
            pltpu.VMEM((rows, channels), BF16),
            pltpu.VMEM((rows, channels), BF16),
            pltpu.VMEM((rows, 3 * channels), BF16),
            pltpu.VMEM((nodes, heads * nodes), F32),
            pltpu.VMEM((128 * heads // channels * nodes, 128), BF16),
            pltpu.VMEM((column_devices, row_devices, 16, width), BF16),
            pltpu.VMEM((column_devices, row_devices, 16, width), BF16),
            pltpu.VMEM((row_devices, 16, width), BF16),
            pltpu.VMEM((row_devices, 16, width), BF16),
            pltpu.VMEM((16, width), BF16),
            pltpu.VMEM((row_devices, 16, width), BF16),
            pltpu.VMEM((column_devices, row_devices, 16, width), BF16),
            dma((count,)),
            dma((count,)),
            dma((column_devices,)),
            dma((row_devices,)),
            dma((row_devices,)),
            dma((column_devices,)),
            dma((chunks,)),
            dma(()),
            dma(()),
            dma((4,)),
        ],
        compiler_params=pltpu.CompilerParams(
            collective_id=0, has_side_effects=True, vmem_limit_bytes=56 * 1024 * 1024
        ),
    )(
        tokens.reshape(shape),
        cotangent.reshape(shape),
        norm1_gain.reshape(1, channels),
        w_qkv,
        w_out,
        pos_bias.reshape(heads * nodes, nodes),
        norm2_gain.reshape(1, channels),
        w_up,
        w_down,
    )
    return (
        mixed.reshape(tokens.shape),
        grad_tokens.reshape(tokens.shape),
        grad_qkv,
        grad_out,
    )


def solution(mesh):
    placed = (P("gy", "gx", None), P("gy", "gx", None), P(), P(), P(), P(), P(), P(), P())
    return jax.shard_map(
        local,
        mesh=mesh,
        in_specs=placed,
        out_specs=(P("gy", "gx", None), P("gy", "gx", None), P(), P()),
        check_vma=False,
    )
```

```python
import functools
import math

import jax
import jax.numpy as jnp
from jax import lax
from jax.experimental import pallas as pl
from jax.experimental.pallas import tpu as pltpu
from jax.sharding import PartitionSpec as P

GRID = 8
MEMBERS = GRID * GRID
EPSILON = 1e-05
BATCH = 16
PIECE = 2 * BATCH
MESH = pl.DeviceIdType.MESH
F32 = jnp.float32
BF16 = jnp.bfloat16


def dot(a, b, da=1, db=0):
    return lax.dot_general(a, b, (((da,), (db,)), ((), ())), preferred_element_type=F32)


def unit_of(wide):
    centre = jnp.mean(wide, axis=-1, keepdims=True)
    shifted = wide - centre
    variance = jnp.mean(shifted * shifted, axis=-1, keepdims=True)
    inverse = lax.rsqrt(variance + EPSILON)
    return shifted * inverse, inverse


def chunk_work(block, result, weights, acc, work, heads):
    gain1, w_qkv, w_out, bias, gain2, w_up, w_down, mask = weights
    wide, xg, gg, normed, qkv, dctx, ctx, dqkv = work
    channels = xg.shape[-1]
    rows = BATCH * MEMBERS
    scale = 1.0 / math.sqrt(channels // heads)
    half = 128

    step = 256

    def regroup():
        for tensor, kept in ((0, xg), (1, gg)):
            value = block[tensor].astype(F32).reshape(rows, channels)
            for part in range(channels // half):
                wide[part] = value[:, part * half : (part + 1) * half]
            for group in range(BATCH):
                for part in range(channels // half):
                    kept[group * MEMBERS : (group + 1) * MEMBERS, part * half : (part + 1) * half] = wide[
                        part, pl.ds(group, MEMBERS, stride=BATCH), :
                    ].astype(BF16)

    def before(index, carry):
        at = pl.ds(pl.multiple_of(index * step, step), step)
        unit, inverse = unit_of(xg[at, :].astype(F32))
        low = (unit * gain1[...]).astype(BF16)
        normed[at, :] = low
        qkv[at, :] = dot(low, w_qkv[...]).astype(BF16)
        dctx[at, :] = dot(gg[at, :], w_out[...], 1, 1).astype(BF16)
        return carry

    lanes = 128
    head_width = channels // heads
    span_heads = lanes // head_width
    span = span_heads * MEMBERS

    def some_heads(at, which):
        first = which * lanes
        query = qkv[at, first : first + lanes]
        keys = qkv[at, channels + first : channels + first + lanes]
        values = qkv[at, 2 * channels + first : 2 * channels + first + lanes]
        spread = mask[...]
        query_wide = jnp.concatenate([query] * span_heads, axis=0) * spread
        d_wide = jnp.concatenate([dctx[at, first : first + lanes]] * span_heads, axis=0) * spread
        scores = dot(keys, query_wide, 1, 1) * scale + bias[:, which * span : (which + 1) * span]
        top = jnp.max(scores, axis=0, keepdims=True)
        raised = jnp.exp(scores - top)
        probs = raised / jnp.sum(raised, axis=0, keepdims=True)
        low = probs.astype(BF16)
        d_probs = dot(values, d_wide, 1, 1)
        inner = jnp.sum(probs * d_probs, axis=0, keepdims=True)
        d_scaled = (probs * (d_probs - inner) * scale).astype(BF16)

        def gathered(left, right):
            full = dot(left, right, 0, 0)
            lane = lax.broadcasted_iota(jnp.int32, (MEMBERS, lanes), 1) // head_width
            total = full[0:MEMBERS]
            for head in range(1, span_heads):
                total = jnp.where(lane == head, full[head * MEMBERS : (head + 1) * MEMBERS], total)
            return total

        ctx[at, first : first + lanes] = gathered(low, values).astype(BF16)
        dqkv[at, first : first + lanes] = gathered(d_scaled, keys).astype(BF16)
        dqkv[at, channels + first : channels + first + lanes] = dot(d_scaled, query_wide).astype(BF16)
        dqkv[at, 2 * channels + first : 2 * channels + first + lanes] = dot(low, d_wide).astype(BF16)

    together = 4

    def attend(index, carry):
        for inner in range(together):
            at = pl.ds(pl.multiple_of((together * index + inner) * MEMBERS, MEMBERS), MEMBERS)
            for which in range(channels // lanes):
                some_heads(at, which)
        return carry

    def attention():
        regroup()
        lax.fori_loop(0, rows // step, before, 0)
        lax.fori_loop(0, BATCH // together, attend, 0)
        acc[:, 0 : 3 * channels] += dot(normed[...], dqkv[...], 0, 0)
        acc[:, 3 * channels : 4 * channels] += dot(ctx[...], gg[...], 0, 0)

    def spread_out(index, value):
        groups = step // MEMBERS
        for local in range(groups):
            for part in range(channels // half):
                wide[part, pl.ds(index * groups + local, MEMBERS, stride=BATCH), :] = value[
                    local * MEMBERS : (local + 1) * MEMBERS, part * half : (part + 1) * half
                ]

    def finish(tensor):
        value = jnp.concatenate([wide[part] for part in range(channels // half)], axis=1)
        result[tensor] = value.reshape(MEMBERS, BATCH, channels).astype(BF16)

    def forward(index, carry):
        at = pl.ds(pl.multiple_of(index * step, step), step)
        attended = (xg[at, :].astype(F32) + dot(ctx[at, :], w_out[...])).astype(BF16).astype(F32)
        unit, inverse = unit_of(attended)
        low = (unit * gain2[...]).astype(BF16)
        hidden = jax.nn.gelu(dot(low, w_up[...])).astype(BF16)
        spread_out(index, attended + dot(hidden, w_down[...]))
        return carry

    def backward(index, carry):
        at = pl.ds(pl.multiple_of(index * step, step), step)
        unit, inverse = unit_of(xg[at, :].astype(F32))
        d_unit = dot(dqkv[at, :], w_qkv[...], 1, 1) * gain1[...]
        d_x = inverse * (
            d_unit
            - jnp.mean(d_unit, axis=-1, keepdims=True)
            - unit * jnp.mean(d_unit * unit, axis=-1, keepdims=True)
        )
        spread_out(index, gg[at, :].astype(F32) + d_x)
        return carry

    def mlp():
        lax.fori_loop(0, rows // step, forward, 0)
        finish(0)

    def token_gradient():
        lax.fori_loop(0, rows // step, backward, 0)
        finish(1)

    return attention, mlp, token_gradient


def kernel(
    plan,
    tokens, cotangent, gain1, w_qkv, w_out, pos_bias, gain2, w_up, w_down,
    results, grad_qkv, grad_out,
    inbox, outbox, acc, wide, xg, gg, normed, qkv, dctx, ctx, dqkv, bias, mask,
    parts, column_parts, column_sum, row_parts, share, row_shares, shares,
    sent_in, sent_out, sent_column, sent_row, sent_row_back, sent_column_back,
    chunk_sem, home_sem, sum_sem,
):
    row_devices, column_devices, row_part, extra, members, splits, strip, per_block, heads, factor = plan
    count = row_devices * column_devices
    gy = lax.axis_index("gy")
    gx = lax.axis_index("gx")
    me = gy * column_devices + gx

    def place(device):
        return device // column_devices, device % column_devices

    def home(device):
        row, column = place(device)
        return row * row_part + column // splits, (column % splits) * strip

    def seat(device):
        row, column = place(device)
        return (row // extra) * GRID + column * members, row % extra

    def peers(body):
        def step(index, carry):
            device = (me + index) % count
            body(index, device, place(device))
            return carry

        lax.fori_loop(1, count, step, 0)

    barrier = pltpu.get_barrier_semaphore()
    peers(lambda index, device, at: pl.semaphore_signal(barrier, inc=1, device_id=at, device_id_type=MESH))
    pl.semaphore_wait(barrier, count - 1)

    my_member, my_extra = seat(me)
    my_row, my_column = home(me)

    pieces = strip // PIECE

    def send_block(piece, _):
        part = my_extra * pieces + piece
        span = pl.ds(my_member, members)

        def source(device, array):
            row, column = home(device)
            return array.at[row, :, pl.ds(pl.multiple_of(column + piece * PIECE, PIECE), PIECE), :]

        for tensor, array in ((0, tokens), (1, cotangent)):
            pltpu.make_async_copy(
                source(me, array), inbox.at[part, tensor, span], chunk_sem.at[part]
            ).start()

        def to_peer(index, device, at):
            for tensor, array in ((0, tokens), (1, cotangent)):
                pltpu.make_async_remote_copy(
                    src_ref=source(device, array),
                    dst_ref=inbox.at[part, tensor, span],
                    send_sem=sent_in.at[index],
                    recv_sem=chunk_sem.at[part],
                    device_id=at,
                    device_id_type=MESH,
                ).start()

        peers(to_peer)
        return _

    lax.fori_loop(0, pieces, send_block, 0)
    acc[...] = jnp.zeros_like(acc)
    bias[...] = pos_bias[...].T
    channels = acc.shape[0]
    mask[...] = (
        lax.broadcasted_iota(jnp.int32, mask.shape, 0) // MEMBERS
        == lax.broadcasted_iota(jnp.int32, mask.shape, 1) // (channels // heads)
    ).astype(F32).astype(BF16)
    weights = (gain1, w_qkv, w_out, bias, gain2, w_up, w_down, mask)
    work = (wide, xg, gg, normed, qkv, dctx, ctx, dqkv)

    def send_home(chunk):
        part = chunk // per_block
        piece = chunk % per_block
        column = pl.ds(pl.multiple_of(my_column + piece * BATCH, BATCH), BATCH)

        def keep():
            pltpu.make_async_copy(
                outbox.at[chunk, :, pl.ds(my_member, members)], results.at[:, my_row, :, column, :], home_sem
            ).start()

        def to_peer(index, device, at):
            member, its = seat(device)

            def send():
                pltpu.make_async_remote_copy(
                    src_ref=outbox.at[chunk, :, pl.ds(member, members)],
                    dst_ref=results.at[:, my_row, :, column, :],
                    send_sem=sent_out.at[index],
                    recv_sem=home_sem,
                    device_id=at,
                    device_id_type=MESH,
                ).start()

            if extra == 1:
                send()
            else:
                pl.when(its == part)(send)

        if extra == 1:
            keep()
        else:
            pl.when(my_extra == part)(keep)
        peers(to_peer)

    def exchange(stage, axis, source, target, sent):
        size, own = ((row_devices, gy), (column_devices, gx))[axis]
        pltpu.make_async_copy(source(own), target.at[own], sum_sem.at[stage]).start()

        def step(index, carry):
            other = (own + index) % size
            pltpu.make_async_remote_copy(
                src_ref=source(other),
                dst_ref=target.at[own],
                send_sem=sent.at[index],
                recv_sem=sum_sem.at[stage],
                device_id=((other, gx), (gy, other))[axis],
                device_id_type=MESH,
            ).start()
            return carry

        lax.fori_loop(1, size, step, 0)

    def arrive(stage, target):
        pltpu.make_async_copy(target, target, sum_sem.at[stage]).wait()

    height, width = share.shape
    across = acc.shape[1] // width

    def areas():
        for place_of in range(count):
            yield (
                place_of // row_devices,
                place_of % row_devices,
                place_of // across * height,
                place_of % across * width,
            )

    chunks = extra * per_block

    halves = PIECE // BATCH

    def one_chunk(chunk, _):
        part = chunk // halves
        at = pl.ds(pl.multiple_of(chunk % halves * BATCH, BATCH), BATCH)

        @pl.when(chunk % halves == 0)
        def piece_here():
            pltpu.make_async_copy(inbox.at[part], inbox.at[part], chunk_sem.at[part]).wait()

        attention, mlp, token_gradient = chunk_work(
            inbox.at[part, :, :, at, :], outbox.at[chunk], weights, acc, work, heads
        )
        attention()

        @pl.when(chunk == chunks - 1)
        def begin_sums():
            for column, row, top, left in areas():
                parts[column, row] = acc[top : top + height, left : left + width].astype(BF16)
            exchange(0, 1, lambda other: parts.at[other], column_parts, sent_column)

        mlp()
        token_gradient()
        pl.when(chunk < chunks - 2)(lambda: send_home(chunk))
        return _

    lax.fori_loop(0, chunks, one_chunk, 0)

    arrive(0, column_parts)
    column_sum[...] = jnp.sum(column_parts[...].astype(F32), axis=0).astype(BF16)
    exchange(1, 0, lambda other: column_sum.at[other], row_parts, sent_row)
    send_home(chunks - 2)
    arrive(1, row_parts)
    share[...] = jnp.sum(row_parts[...].astype(F32), axis=0).astype(BF16)
    exchange(2, 0, lambda other: share, row_shares, sent_row_back)
    send_home(chunks - 1)
    arrive(2, row_shares)
    exchange(3, 1, lambda other: row_shares, shares, sent_column_back)
    arrive(3, shares)
    for column, row, top, left in areas():
        value = shares[column, row].astype(F32) * factor
        cut = min(max(3 * channels - left, 0), width)
        if cut > 0:
            grad_qkv[top : top + height, left : left + cut] = value[:, :cut]
        if cut < width:
            start = left + cut - 3 * channels
            grad_out[top : top + height, start : start + width - cut] = value[:, cut:]

    def drain(index, device, at):
        moved = outbox.at[pl.ds(0, per_block), :, pl.ds(0, members)]
        pltpu.make_async_copy(moved, moved, sent_in.at[index]).wait()
        pltpu.make_async_copy(moved, moved, sent_out.at[index]).wait()

    peers(drain)
    for sent, size, moved in (
        (sent_column, column_devices, row_parts),
        (sent_row, row_devices, share),
        (sent_row_back, row_devices, share),
        (sent_column_back, column_devices, row_parts),
    ):
        for index in range(1, size):
            pltpu.make_async_copy(moved, moved, sent.at[index]).wait()
    pltpu.make_async_copy(results, results, home_sem).wait()


def local(tokens, cotangent, norm1_gain, w_qkv, w_out, pos_bias, norm2_gain, w_up, w_down):
    tile_rows, tile_cols, channels = tokens.shape
    row_devices = lax.axis_size("gy")
    column_devices = lax.axis_size("gx")
    count = row_devices * column_devices
    heads, nodes = pos_bias.shape[:2]
    row_part = tile_rows // row_devices
    extra = row_devices // GRID
    members = GRID // column_devices
    stride = tile_cols // members
    splits = column_devices // row_part
    strip = stride // splits
    per_block = strip // BATCH
    chunks = extra * per_block
    factor = 1.0 / math.sqrt(tile_rows * tile_cols * count)
    plan = (row_devices, column_devices, row_part, extra, members, splits, strip, per_block, heads, factor)
    shape = (tile_rows, members, stride, channels)
    rows = BATCH * MEMBERS
    width = 4 * channels * channels // (16 * count)
    anywhere = pl.BlockSpec(memory_space=pl.ANY)
    vmem = pl.BlockSpec(memory_space=pltpu.VMEM)
    dma = pltpu.SemaphoreType.DMA
    inward = (extra * strip // PIECE, 2, MEMBERS, PIECE, channels)
    outward = (chunks, 2, MEMBERS, BATCH, channels)
    results, grad_qkv, grad_out = pl.pallas_call(
        functools.partial(kernel, plan),
        out_shape=(
            jax.ShapeDtypeStruct((2,) + shape, BF16),
            jax.ShapeDtypeStruct((channels, 3 * channels), F32),
            jax.ShapeDtypeStruct((channels, channels), F32),
        ),
        in_specs=[anywhere, anywhere] + [vmem] * 7,
        out_specs=(anywhere, vmem, vmem),
        scratch_shapes=[
            pltpu.VMEM(inward, BF16),
            pltpu.VMEM(outward, BF16),
            pltpu.VMEM((channels, 4 * channels), F32),
            pltpu.VMEM((channels // 128, rows, 128), F32),
            pltpu.VMEM((rows, channels), BF16),
            pltpu.VMEM((rows, channels), BF16),
            pltpu.VMEM((rows, channels), BF16),
            pltpu.VMEM((rows, 3 * channels), BF16),
            pltpu.VMEM((rows, channels), BF16),
            pltpu.VMEM((rows, channels), BF16),
            pltpu.VMEM((rows, 3 * channels), BF16),
            pltpu.VMEM((nodes, heads * nodes), F32),
            pltpu.VMEM((128 * heads // channels * nodes, 128), BF16),
            pltpu.VMEM((column_devices, row_devices, 16, width), BF16),
            pltpu.VMEM((column_devices, row_devices, 16, width), BF16),
            pltpu.VMEM((row_devices, 16, width), BF16),
            pltpu.VMEM((row_devices, 16, width), BF16),
            pltpu.VMEM((16, width), BF16),
            pltpu.VMEM((row_devices, 16, width), BF16),
            pltpu.VMEM((column_devices, row_devices, 16, width), BF16),
            dma((count,)),
            dma((count,)),
            dma((column_devices,)),
            dma((row_devices,)),
            dma((row_devices,)),
            dma((column_devices,)),
            dma((inward[0],)),
            dma(()),
            dma((4,)),
        ],
        compiler_params=pltpu.CompilerParams(
            collective_id=0, has_side_effects=True, vmem_limit_bytes=56 * 1024 * 1024
        ),
    )(
        tokens.reshape(shape),
        cotangent.reshape(shape),
        norm1_gain.reshape(1, channels),
        w_qkv,
        w_out,
        pos_bias.reshape(heads * nodes, nodes),
        norm2_gain.reshape(1, channels),
        w_up,
        w_down,
    )
    return (
        results[0].reshape(tokens.shape),
        results[1].reshape(tokens.shape),
        grad_qkv,
        grad_out,
    )


def solution(mesh):
    placed = (P("gy", "gx", None), P("gy", "gx", None), P(), P(), P(), P(), P(), P(), P())
    return jax.shard_map(
        local,
        mesh=mesh,
        in_specs=placed,
        out_specs=(P("gy", "gx", None), P("gy", "gx", None), P(), P()),
        check_vma=False,
    )
```

```python
import functools
import math

import jax
import jax.numpy as jnp
from jax import lax
from jax.experimental import pallas as pl
from jax.experimental.pallas import tpu as pltpu
from jax.sharding import PartitionSpec as P

GRID = 8
MEMBERS = GRID * GRID
EPSILON = 1e-05
BATCH = 16
MESH = pl.DeviceIdType.MESH
F32 = jnp.float32
BF16 = jnp.bfloat16


def dot(a, b, da=1, db=0):
    return lax.dot_general(a, b, (((da,), (db,)), ((), ())), preferred_element_type=F32)


def unit_of(wide):
    centre = jnp.mean(wide, axis=-1, keepdims=True)
    shifted = wide - centre
    variance = jnp.mean(shifted * shifted, axis=-1, keepdims=True)
    inverse = lax.rsqrt(variance + EPSILON)
    return shifted * inverse, inverse


def chunk_work(block, result, weights, acc, work, heads):
    gain1, w_qkv, w_out, bias, gain2, w_up, w_down, mask = weights
    wide, xg, gg, normed, qkv, dctx, ctx, dqkv = work
    channels = xg.shape[-1]
    rows = BATCH * MEMBERS
    scale = 1.0 / math.sqrt(channels // heads)
    half = 128

    step = 256

    def regroup():
        for tensor, kept in ((0, xg), (1, gg)):
            value = block[tensor].astype(F32).reshape(rows, channels)
            for part in range(channels // half):
                wide[part] = value[:, part * half : (part + 1) * half]
            for group in range(BATCH):
                for part in range(channels // half):
                    kept[group * MEMBERS : (group + 1) * MEMBERS, part * half : (part + 1) * half] = wide[
                        part, pl.ds(group, MEMBERS, stride=BATCH), :
                    ].astype(BF16)

    def before(index, carry):
        at = pl.ds(pl.multiple_of(index * step, step), step)
        unit, inverse = unit_of(xg[at, :].astype(F32))
        low = (unit * gain1[...]).astype(BF16)
        normed[at, :] = low
        qkv[at, :] = dot(low, w_qkv[...]).astype(BF16)
        dctx[at, :] = dot(gg[at, :], w_out[...], 1, 1).astype(BF16)
        return carry

    lanes = 128
    head_width = channels // heads
    span_heads = lanes // head_width
    span = span_heads * MEMBERS

    def some_heads(at, which):
        first = which * lanes
        query = qkv[at, first : first + lanes]
        keys = qkv[at, channels + first : channels + first + lanes]
        values = qkv[at, 2 * channels + first : 2 * channels + first + lanes]
        spread = mask[...]
        query_wide = jnp.concatenate([query] * span_heads, axis=0) * spread
        d_wide = jnp.concatenate([dctx[at, first : first + lanes]] * span_heads, axis=0) * spread
        scores = dot(keys, query_wide, 1, 1) * scale + bias[:, which * span : (which + 1) * span]
        top = jnp.max(scores, axis=0, keepdims=True)
        raised = jnp.exp(scores - top)
        probs = raised / jnp.sum(raised, axis=0, keepdims=True)
        low = probs.astype(BF16)
        d_probs = dot(values, d_wide, 1, 1)
        inner = jnp.sum(probs * d_probs, axis=0, keepdims=True)
        d_scaled = (probs * (d_probs - inner) * scale).astype(BF16)

        def gathered(left, right):
            full = dot(left, right, 0, 0)
            lane = lax.broadcasted_iota(jnp.int32, (MEMBERS, lanes), 1) // head_width
            total = full[0:MEMBERS]
            for head in range(1, span_heads):
                total = jnp.where(lane == head, full[head * MEMBERS : (head + 1) * MEMBERS], total)
            return total

        ctx[at, first : first + lanes] = gathered(low, values).astype(BF16)
        dqkv[at, first : first + lanes] = gathered(d_scaled, keys).astype(BF16)
        dqkv[at, channels + first : channels + first + lanes] = dot(d_scaled, query_wide).astype(BF16)
        dqkv[at, 2 * channels + first : 2 * channels + first + lanes] = dot(low, d_wide).astype(BF16)

    together = 4

    def attend(index, carry):
        for inner in range(together):
            at = pl.ds(pl.multiple_of((together * index + inner) * MEMBERS, MEMBERS), MEMBERS)
            for which in range(channels // lanes):
                some_heads(at, which)
        return carry

    def attention():
        regroup()
        lax.fori_loop(0, rows // step, before, 0)
        lax.fori_loop(0, BATCH // together, attend, 0)
        acc[:, 0 : 3 * channels] += dot(normed[...], dqkv[...], 0, 0)
        acc[:, 3 * channels : 4 * channels] += dot(ctx[...], gg[...], 0, 0)

    def spread_out(index, value):
        groups = step // MEMBERS
        for local in range(groups):
            for part in range(channels // half):
                wide[part, pl.ds(index * groups + local, MEMBERS, stride=BATCH), :] = value[
                    local * MEMBERS : (local + 1) * MEMBERS, part * half : (part + 1) * half
                ]

    def finish(tensor):
        value = jnp.concatenate([wide[part] for part in range(channels // half)], axis=1)
        result[tensor] = value.reshape(MEMBERS, BATCH, channels).astype(BF16)

    def forward(index, carry):
        at = pl.ds(pl.multiple_of(index * step, step), step)
        attended = (xg[at, :].astype(F32) + dot(ctx[at, :], w_out[...])).astype(BF16).astype(F32)
        unit, inverse = unit_of(attended)
        low = (unit * gain2[...]).astype(BF16)
        hidden = jax.nn.gelu(dot(low, w_up[...])).astype(BF16)
        spread_out(index, attended + dot(hidden, w_down[...]))
        return carry

    def backward(index, carry):
        at = pl.ds(pl.multiple_of(index * step, step), step)
        unit, inverse = unit_of(xg[at, :].astype(F32))
        d_unit = dot(dqkv[at, :], w_qkv[...], 1, 1) * gain1[...]
        d_x = inverse * (
            d_unit
            - jnp.mean(d_unit, axis=-1, keepdims=True)
            - unit * jnp.mean(d_unit * unit, axis=-1, keepdims=True)
        )
        spread_out(index, gg[at, :].astype(F32) + d_x)
        return carry

    def mlp():
        lax.fori_loop(0, rows // step, forward, 0)
        finish(0)

    def token_gradient():
        lax.fori_loop(0, rows // step, backward, 0)
        finish(1)

    return attention, mlp, token_gradient


def kernel(
    plan,
    tokens, cotangent, gain1, w_qkv, w_out, pos_bias, gain2, w_up, w_down,
    mixed, grad_tokens, grad_qkv, grad_out,
    inbox, outbox, acc, wide, xg, gg, normed, qkv, dctx, ctx, dqkv, bias, mask,
    parts, column_parts, column_sum, row_parts, share, row_shares, shares,
    sent_in, sent_out, sent_column, sent_row, sent_row_back, sent_column_back,
    chunk_sem, mixed_sem, grad_sem, sum_sem,
):
    row_devices, column_devices, row_part, extra, members, splits, strip, per_block, heads, factor = plan
    count = row_devices * column_devices
    gy = lax.axis_index("gy")
    gx = lax.axis_index("gx")
    me = gy * column_devices + gx

    def place(device):
        return device // column_devices, device % column_devices

    def home(device):
        row, column = place(device)
        return row * row_part + column // splits, (column % splits) * strip

    def seat(device):
        row, column = place(device)
        return (row // extra) * GRID + column * members, row % extra

    def peers(body):
        def step(index, carry):
            device = (me + index) % count
            body(index, device, place(device))
            return carry

        lax.fori_loop(1, count, step, 0)

    barrier = pltpu.get_barrier_semaphore()
    peers(lambda index, device, at: pl.semaphore_signal(barrier, inc=1, device_id=at, device_id_type=MESH))
    pl.semaphore_wait(barrier, count - 1)

    my_member, my_extra = seat(me)
    my_row, my_column = home(me)

    def send_block(piece, _):
        chunk = my_extra * per_block + piece
        span = pl.ds(my_member, members)

        def source(device, array):
            row, column = home(device)
            return array.at[row, :, pl.ds(pl.multiple_of(column + piece * BATCH, BATCH), BATCH), :]

        for tensor, array in ((0, tokens), (1, cotangent)):
            pltpu.make_async_copy(
                source(me, array), inbox.at[chunk, tensor, span], chunk_sem.at[chunk]
            ).start()

        def to_peer(index, device, at):
            for tensor, array in ((0, tokens), (1, cotangent)):
                pltpu.make_async_remote_copy(
                    src_ref=source(device, array),
                    dst_ref=inbox.at[chunk, tensor, span],
                    send_sem=sent_in.at[index],
                    recv_sem=chunk_sem.at[chunk],
                    device_id=at,
                    device_id_type=MESH,
                ).start()

        peers(to_peer)
        return _

    lax.fori_loop(0, per_block, send_block, 0)
    acc[...] = jnp.zeros_like(acc)
    bias[...] = pos_bias[...].T
    channels = acc.shape[0]
    mask[...] = (
        lax.broadcasted_iota(jnp.int32, mask.shape, 0) // MEMBERS
        == lax.broadcasted_iota(jnp.int32, mask.shape, 1) // (channels // heads)
    ).astype(F32).astype(BF16)
    weights = (gain1, w_qkv, w_out, bias, gain2, w_up, w_down, mask)
    work = (wide, xg, gg, normed, qkv, dctx, ctx, dqkv)
    targets = ((mixed, mixed_sem), (grad_tokens, grad_sem))

    def send_home(chunk, tensor):
        part = chunk // per_block
        piece = chunk % per_block
        column = pl.ds(pl.multiple_of(my_column + piece * BATCH, BATCH), BATCH)
        array, sem = targets[tensor]

        def keep():
            pltpu.make_async_copy(
                outbox.at[chunk, tensor, pl.ds(my_member, members)], array.at[my_row, :, column, :], sem
            ).start()

        def to_peer(index, device, at):
            member, its = seat(device)

            def send():
                pltpu.make_async_remote_copy(
                    src_ref=outbox.at[chunk, tensor, pl.ds(member, members)],
                    dst_ref=array.at[my_row, :, column, :],
                    send_sem=sent_out.at[index],
                    recv_sem=sem,
                    device_id=at,
                    device_id_type=MESH,
                ).start()

            if extra == 1:
                send()
            else:
                pl.when(its == part)(send)

        if extra == 1:
            keep()
        else:
            pl.when(my_extra == part)(keep)
        peers(to_peer)

    def exchange(stage, axis, source, target, sent):
        size, own = ((row_devices, gy), (column_devices, gx))[axis]
        pltpu.make_async_copy(source(own), target.at[own], sum_sem.at[stage]).start()

        def step(index, carry):
            other = (own + index) % size
            pltpu.make_async_remote_copy(
                src_ref=source(other),
                dst_ref=target.at[own],
                send_sem=sent.at[index],
                recv_sem=sum_sem.at[stage],
                device_id=((other, gx), (gy, other))[axis],
                device_id_type=MESH,
            ).start()
            return carry

        lax.fori_loop(1, size, step, 0)

    def arrive(stage, target):
        pltpu.make_async_copy(target, target, sum_sem.at[stage]).wait()

    height, width = share.shape
    across = acc.shape[1] // width

    def areas():
        for place_of in range(count):
            yield (
                place_of // row_devices,
                place_of % row_devices,
                place_of // across * height,
                place_of % across * width,
            )

    chunks = extra * per_block

    def one_chunk(chunk, _):
        pltpu.make_async_copy(inbox.at[chunk], inbox.at[chunk], chunk_sem.at[chunk]).wait()
        attention, mlp, token_gradient = chunk_work(
            inbox.at[chunk], outbox.at[chunk], weights, acc, work, heads
        )
        attention()

        @pl.when(chunk == chunks - 1)
        def begin_sums():
            for column, row, top, left in areas():
                parts[column, row] = acc[top : top + height, left : left + width].astype(BF16)
            exchange(0, 1, lambda other: parts.at[other], column_parts, sent_column)
            send_home(chunks - 2, 0)

        mlp()
        pl.when(chunk < chunks - 2)(lambda: send_home(chunk, 0))
        token_gradient()
        pl.when(chunk < chunks - 2)(lambda: send_home(chunk, 1))
        return _

    lax.fori_loop(0, chunks, one_chunk, 0)

    arrive(0, column_parts)
    column_sum[...] = jnp.sum(column_parts[...].astype(F32), axis=0).astype(BF16)
    exchange(1, 0, lambda other: column_sum.at[other], row_parts, sent_row)
    send_home(chunks - 2, 1)
    arrive(1, row_parts)
    share[...] = jnp.sum(row_parts[...].astype(F32), axis=0).astype(BF16)
    exchange(2, 0, lambda other: share, row_shares, sent_row_back)
    send_home(chunks - 1, 0)
    arrive(2, row_shares)
    exchange(3, 1, lambda other: row_shares, shares, sent_column_back)
    send_home(chunks - 1, 1)
    arrive(3, shares)
    for column, row, top, left in areas():
        value = shares[column, row].astype(F32) * factor
        cut = min(max(3 * channels - left, 0), width)
        if cut > 0:
            grad_qkv[top : top + height, left : left + cut] = value[:, :cut]
        if cut < width:
            start = left + cut - 3 * channels
            grad_out[top : top + height, start : start + width - cut] = value[:, cut:]

    def drain(index, device, at):
        moved = inbox.at[pl.ds(0, per_block), :, pl.ds(0, members)]
        pltpu.make_async_copy(moved, moved, sent_in.at[index]).wait()
        pltpu.make_async_copy(moved, moved, sent_out.at[index]).wait()

    peers(drain)
    for sent, size, moved in (
        (sent_column, column_devices, row_parts),
        (sent_row, row_devices, share),
        (sent_row_back, row_devices, share),
        (sent_column_back, column_devices, row_parts),
    ):
        for index in range(1, size):
            pltpu.make_async_copy(moved, moved, sent.at[index]).wait()
    pltpu.make_async_copy(mixed, mixed, mixed_sem).wait()
    pltpu.make_async_copy(grad_tokens, grad_tokens, grad_sem).wait()


def local(tokens, cotangent, norm1_gain, w_qkv, w_out, pos_bias, norm2_gain, w_up, w_down):
    tile_rows, tile_cols, channels = tokens.shape
    row_devices = lax.axis_size("gy")
    column_devices = lax.axis_size("gx")
    count = row_devices * column_devices
    heads, nodes = pos_bias.shape[:2]
    row_part = tile_rows // row_devices
    extra = row_devices // GRID
    members = GRID // column_devices
    stride = tile_cols // members
    splits = column_devices // row_part
    strip = stride // splits
    per_block = strip // BATCH
    chunks = extra * per_block
    factor = 1.0 / math.sqrt(tile_rows * tile_cols * count)
    plan = (row_devices, column_devices, row_part, extra, members, splits, strip, per_block, heads, factor)
    shape = (tile_rows, members, stride, channels)
    rows = BATCH * MEMBERS
    width = 4 * channels * channels // (16 * count)
    anywhere = pl.BlockSpec(memory_space=pl.ANY)
    vmem = pl.BlockSpec(memory_space=pltpu.VMEM)
    dma = pltpu.SemaphoreType.DMA
    box = (chunks, 2, MEMBERS, BATCH, channels)
    mixed, grad_tokens, grad_qkv, grad_out = pl.pallas_call(
        functools.partial(kernel, plan),
        out_shape=(
            jax.ShapeDtypeStruct(shape, BF16),
            jax.ShapeDtypeStruct(shape, BF16),
            jax.ShapeDtypeStruct((channels, 3 * channels), F32),
            jax.ShapeDtypeStruct((channels, channels), F32),
        ),
        in_specs=[anywhere, anywhere] + [vmem] * 7,
        out_specs=(anywhere, anywhere, vmem, vmem),
        scratch_shapes=[
            pltpu.VMEM(box, BF16),
            pltpu.VMEM(box, BF16),
            pltpu.VMEM((channels, 4 * channels), F32),
            pltpu.VMEM((channels // 128, rows, 128), F32),
            pltpu.VMEM((rows, channels), BF16),
            pltpu.VMEM((rows, channels), BF16),
            pltpu.VMEM((rows, channels), BF16),
            pltpu.VMEM((rows, 3 * channels), BF16),
            pltpu.VMEM((rows, channels), BF16),
            pltpu.VMEM((rows, channels), BF16),
            pltpu.VMEM((rows, 3 * channels), BF16),
            pltpu.VMEM((nodes, heads * nodes), F32),
            pltpu.VMEM((128 * heads // channels * nodes, 128), BF16),
            pltpu.VMEM((column_devices, row_devices, 16, width), BF16),
            pltpu.VMEM((column_devices, row_devices, 16, width), BF16),
            pltpu.VMEM((row_devices, 16, width), BF16),
            pltpu.VMEM((row_devices, 16, width), BF16),
            pltpu.VMEM((16, width), BF16),
            pltpu.VMEM((row_devices, 16, width), BF16),
            pltpu.VMEM((column_devices, row_devices, 16, width), BF16),
            dma((count,)),
            dma((count,)),
            dma((column_devices,)),
            dma((row_devices,)),
            dma((row_devices,)),
            dma((column_devices,)),
            dma((chunks,)),
            dma(()),
            dma(()),
            dma((4,)),
        ],
        compiler_params=pltpu.CompilerParams(
            collective_id=0, has_side_effects=True, vmem_limit_bytes=56 * 1024 * 1024
        ),
    )(
        tokens.reshape(shape),
        cotangent.reshape(shape),
        norm1_gain.reshape(1, channels),
        w_qkv,
        w_out,
        pos_bias.reshape(heads * nodes, nodes),
        norm2_gain.reshape(1, channels),
        w_up,
        w_down,
    )
    return (
        mixed.reshape(tokens.shape),
        grad_tokens.reshape(tokens.shape),
        grad_qkv,
        grad_out,
    )


def solution(mesh):
    placed = (P("gy", "gx", None), P("gy", "gx", None), P(), P(), P(), P(), P(), P(), P())
    return jax.shard_map(
        local,
        mesh=mesh,
        in_specs=placed,
        out_specs=(P("gy", "gx", None), P("gy", "gx", None), P(), P()),
        check_vma=False,
    )
```

```python
import functools
import math

import jax
import jax.numpy as jnp
from jax import lax
from jax.experimental import pallas as pl
from jax.experimental.pallas import tpu as pltpu
from jax.sharding import PartitionSpec as P

GRID = 8
MEMBERS = GRID * GRID
EPSILON = 1e-05
BATCH = 16
MESH = pl.DeviceIdType.MESH
F32 = jnp.float32
BF16 = jnp.bfloat16


def dot(a, b, da=1, db=0):
    return lax.dot_general(a, b, (((da,), (db,)), ((), ())), preferred_element_type=F32)


def unit_of(wide):
    centre = jnp.mean(wide, axis=-1, keepdims=True)
    shifted = wide - centre
    variance = jnp.mean(shifted * shifted, axis=-1, keepdims=True)
    inverse = lax.rsqrt(variance + EPSILON)
    return shifted * inverse, inverse


def chunk_work(block, result, weights, acc, work, heads):
    gain1, w_qkv, w_out, bias, gain2, w_up, w_down, mask = weights
    wide, xg, gg, normed, qkv, dctx, ctx, dqkv = work
    channels = xg.shape[-1]
    rows = BATCH * MEMBERS
    scale = 1.0 / math.sqrt(channels // heads)
    half = 128

    step = 256

    def regroup():
        for tensor, kept in ((0, xg), (1, gg)):
            value = block[tensor].astype(F32).reshape(rows, channels)
            for part in range(channels // half):
                wide[part] = value[:, part * half : (part + 1) * half]
            for group in range(BATCH):
                for part in range(channels // half):
                    kept[group * MEMBERS : (group + 1) * MEMBERS, part * half : (part + 1) * half] = wide[
                        part, pl.ds(group, MEMBERS, stride=BATCH), :
                    ].astype(BF16)

    def before(index, carry):
        at = pl.ds(pl.multiple_of(index * step, step), step)
        unit, inverse = unit_of(xg[at, :].astype(F32))
        low = (unit * gain1[...]).astype(BF16)
        normed[at, :] = low
        qkv[at, :] = dot(low, w_qkv[...]).astype(BF16)
        dctx[at, :] = dot(gg[at, :], w_out[...], 1, 1).astype(BF16)
        return carry

    lanes = 128
    head_width = channels // heads
    span_heads = lanes // head_width
    span = span_heads * MEMBERS

    def some_heads(at, which):
        first = which * lanes
        query = qkv[at, first : first + lanes]
        keys = qkv[at, channels + first : channels + first + lanes]
        values = qkv[at, 2 * channels + first : 2 * channels + first + lanes]
        spread = mask[...]
        query_wide = jnp.concatenate([query] * span_heads, axis=0) * spread
        d_wide = jnp.concatenate([dctx[at, first : first + lanes]] * span_heads, axis=0) * spread
        scores = dot(keys, query_wide, 1, 1) * scale + bias[:, which * span : (which + 1) * span]
        top = jnp.max(scores, axis=0, keepdims=True)
        raised = jnp.exp(scores - top)
        probs = raised / jnp.sum(raised, axis=0, keepdims=True)
        low = probs.astype(BF16)
        d_probs = dot(values, d_wide, 1, 1)
        inner = jnp.sum(probs * d_probs, axis=0, keepdims=True)
        d_scaled = (probs * (d_probs - inner) * scale).astype(BF16)

        def gathered(left, right):
            full = dot(left, right, 0, 0)
            lane = lax.broadcasted_iota(jnp.int32, (MEMBERS, lanes), 1) // head_width
            total = full[0:MEMBERS]
            for head in range(1, span_heads):
                total = jnp.where(lane == head, full[head * MEMBERS : (head + 1) * MEMBERS], total)
            return total

        ctx[at, first : first + lanes] = gathered(low, values).astype(BF16)
        dqkv[at, first : first + lanes] = gathered(d_scaled, keys).astype(BF16)
        dqkv[at, channels + first : channels + first + lanes] = dot(d_scaled, query_wide).astype(BF16)
        dqkv[at, 2 * channels + first : 2 * channels + first + lanes] = dot(low, d_wide).astype(BF16)

    together = 4

    def attend(index, carry):
        for inner in range(together):
            at = pl.ds(pl.multiple_of((together * index + inner) * MEMBERS, MEMBERS), MEMBERS)
            for which in range(channels // lanes):
                some_heads(at, which)
        return carry

    def attention():
        regroup()
        lax.fori_loop(0, rows // step, before, 0)
        lax.fori_loop(0, BATCH // together, attend, 0)
        acc[:, 0 : 3 * channels] += dot(normed[...], dqkv[...], 0, 0)
        acc[:, 3 * channels : 4 * channels] += dot(ctx[...], gg[...], 0, 0)

    def spread_out(index, value):
        groups = step // MEMBERS
        for local in range(groups):
            for part in range(channels // half):
                wide[part, pl.ds(index * groups + local, MEMBERS, stride=BATCH), :] = value[
                    local * MEMBERS : (local + 1) * MEMBERS, part * half : (part + 1) * half
                ]

    def finish(tensor):
        value = jnp.concatenate([wide[part] for part in range(channels // half)], axis=1)
        result[tensor] = value.reshape(MEMBERS, BATCH, channels).astype(BF16)

    def forward(index, carry):
        at = pl.ds(pl.multiple_of(index * step, step), step)
        attended = (xg[at, :].astype(F32) + dot(ctx[at, :], w_out[...])).astype(BF16).astype(F32)
        unit, inverse = unit_of(attended)
        low = (unit * gain2[...]).astype(BF16)
        hidden = jax.nn.gelu(dot(low, w_up[...])).astype(BF16)
        spread_out(index, attended + dot(hidden, w_down[...]))
        return carry

    def backward(index, carry):
        at = pl.ds(pl.multiple_of(index * step, step), step)
        unit, inverse = unit_of(xg[at, :].astype(F32))
        d_unit = dot(dqkv[at, :], w_qkv[...], 1, 1) * gain1[...]
        d_x = inverse * (
            d_unit
            - jnp.mean(d_unit, axis=-1, keepdims=True)
            - unit * jnp.mean(d_unit * unit, axis=-1, keepdims=True)
        )
        spread_out(index, gg[at, :].astype(F32) + d_x)
        return carry

    def mlp():
        lax.fori_loop(0, rows // step, forward, 0)
        finish(0)

    def token_gradient():
        lax.fori_loop(0, rows // step, backward, 0)
        finish(1)

    return attention, mlp, token_gradient


def kernel(
    plan,
    tokens, cotangent, gain1, w_qkv, w_out, pos_bias, gain2, w_up, w_down,
    mixed, grad_tokens, grad_qkv, grad_out,
    inbox, outbox, acc, wide, xg, gg, normed, qkv, dctx, ctx, dqkv, bias, mask,
    parts, column_parts, column_sum, row_parts, share, row_shares, shares,
    sent_in, sent_out, sent_column, sent_row, sent_row_back, sent_column_back,
    chunk_sem, mixed_sem, grad_sem, sum_sem,
):
    row_devices, column_devices, row_part, extra, members, splits, strip, per_block, heads, factor = plan
    count = row_devices * column_devices
    gy = lax.axis_index("gy")
    gx = lax.axis_index("gx")
    me = gy * column_devices + gx

    def place(device):
        return device // column_devices, device % column_devices

    def home(device):
        row, column = place(device)
        return row * row_part + column // splits, (column % splits) * strip

    def seat(device):
        row, column = place(device)
        return (row // extra) * GRID + column * members, row % extra

    def peers(body):
        def step(index, carry):
            device = (me + index) % count
            body(index, device, place(device))
            return carry

        lax.fori_loop(1, count, step, 0)

    barrier = pltpu.get_barrier_semaphore()
    peers(lambda index, device, at: pl.semaphore_signal(barrier, inc=1, device_id=at, device_id_type=MESH))
    pl.semaphore_wait(barrier, count - 1)

    my_member, my_extra = seat(me)
    my_row, my_column = home(me)

    def send_block(piece, _):
        chunk = my_extra * per_block + piece
        span = pl.ds(my_member, members)

        def source(device, array):
            row, column = home(device)
            return array.at[row, :, pl.ds(pl.multiple_of(column + piece * BATCH, BATCH), BATCH), :]

        for tensor, array in ((0, tokens), (1, cotangent)):
            pltpu.make_async_copy(
                source(me, array), inbox.at[chunk, tensor, span], chunk_sem.at[chunk]
            ).start()

        def to_peer(index, device, at):
            for tensor, array in ((0, tokens), (1, cotangent)):
                pltpu.make_async_remote_copy(
                    src_ref=source(device, array),
                    dst_ref=inbox.at[chunk, tensor, span],
                    send_sem=sent_in.at[index],
                    recv_sem=chunk_sem.at[chunk],
                    device_id=at,
                    device_id_type=MESH,
                ).start()

        peers(to_peer)
        return _

    lax.fori_loop(0, per_block, send_block, 0)
    acc[...] = jnp.zeros_like(acc)
    bias[...] = pos_bias[...].T
    channels = acc.shape[0]
    mask[...] = (
        lax.broadcasted_iota(jnp.int32, mask.shape, 0) // MEMBERS
        == lax.broadcasted_iota(jnp.int32, mask.shape, 1) // (channels // heads)
    ).astype(F32).astype(BF16)
    weights = (gain1, w_qkv, w_out, bias, gain2, w_up, w_down, mask)
    work = (wide, xg, gg, normed, qkv, dctx, ctx, dqkv)
    targets = ((mixed, mixed_sem), (grad_tokens, grad_sem))

    def send_home(chunk, tensor):
        part = chunk // per_block
        piece = chunk % per_block
        column = pl.ds(pl.multiple_of(my_column + piece * BATCH, BATCH), BATCH)
        array, sem = targets[tensor]

        def keep():
            pltpu.make_async_copy(
                outbox.at[chunk, tensor, pl.ds(my_member, members)], array.at[my_row, :, column, :], sem
            ).start()

        def to_peer(index, device, at):
            member, its = seat(device)

            def send():
                pltpu.make_async_remote_copy(
                    src_ref=outbox.at[chunk, tensor, pl.ds(member, members)],
                    dst_ref=array.at[my_row, :, column, :],
                    send_sem=sent_out.at[index],
                    recv_sem=sem,
                    device_id=at,
                    device_id_type=MESH,
                ).start()

            if extra == 1:
                send()
            else:
                pl.when(its == part)(send)

        if extra == 1:
            keep()
        else:
            pl.when(my_extra == part)(keep)
        peers(to_peer)

    def exchange(stage, axis, source, target, sent):
        size, own = ((row_devices, gy), (column_devices, gx))[axis]
        pltpu.make_async_copy(source(own), target.at[own], sum_sem.at[stage]).start()

        def step(index, carry):
            other = (own + index) % size
            pltpu.make_async_remote_copy(
                src_ref=source(other),
                dst_ref=target.at[own],
                send_sem=sent.at[index],
                recv_sem=sum_sem.at[stage],
                device_id=((other, gx), (gy, other))[axis],
                device_id_type=MESH,
            ).start()
            return carry

        lax.fori_loop(1, size, step, 0)

    def arrive(stage, target):
        pltpu.make_async_copy(target, target, sum_sem.at[stage]).wait()

    height, width = share.shape
    across = acc.shape[1] // width

    def areas():
        for place_of in range(count):
            yield (
                place_of // row_devices,
                place_of % row_devices,
                place_of // across * height,
                place_of % across * width,
            )

    chunks = extra * per_block

    def one_chunk(chunk, _):
        pltpu.make_async_copy(inbox.at[chunk], inbox.at[chunk], chunk_sem.at[chunk]).wait()
        attention, mlp, token_gradient = chunk_work(
            inbox.at[chunk], outbox.at[chunk], weights, acc, work, heads
        )
        attention()

        @pl.when(chunk == chunks - 1)
        def begin_sums():
            for column, row, top, left in areas():
                parts[column, row] = acc[top : top + height, left : left + width].astype(BF16)
            exchange(0, 1, lambda other: parts.at[other], column_parts, sent_column)

        mlp()
        pl.when(chunk < chunks - 1)(lambda: send_home(chunk, 0))
        token_gradient()
        pl.when(chunk < chunks - 2)(lambda: send_home(chunk, 1))
        return _

    lax.fori_loop(0, chunks, one_chunk, 0)

    arrive(0, column_parts)
    column_sum[...] = jnp.sum(column_parts[...].astype(F32), axis=0).astype(BF16)
    exchange(1, 0, lambda other: column_sum.at[other], row_parts, sent_row)
    send_home(chunks - 2, 1)
    arrive(1, row_parts)
    share[...] = jnp.sum(row_parts[...].astype(F32), axis=0).astype(BF16)
    exchange(2, 0, lambda other: share, row_shares, sent_row_back)
    send_home(chunks - 1, 0)
    arrive(2, row_shares)
    exchange(3, 1, lambda other: row_shares, shares, sent_column_back)
    send_home(chunks - 1, 1)
    arrive(3, shares)
    for column, row, top, left in areas():
        value = shares[column, row].astype(F32) * factor
        cut = min(max(3 * channels - left, 0), width)
        if cut > 0:
            grad_qkv[top : top + height, left : left + cut] = value[:, :cut]
        if cut < width:
            start = left + cut - 3 * channels
            grad_out[top : top + height, start : start + width - cut] = value[:, cut:]

    def drain(index, device, at):
        moved = inbox.at[pl.ds(0, per_block), :, pl.ds(0, members)]
        pltpu.make_async_copy(moved, moved, sent_in.at[index]).wait()
        pltpu.make_async_copy(moved, moved, sent_out.at[index]).wait()

    peers(drain)
    for sent, size, moved in (
        (sent_column, column_devices, row_parts),
        (sent_row, row_devices, share),
        (sent_row_back, row_devices, share),
        (sent_column_back, column_devices, row_parts),
    ):
        for index in range(1, size):
            pltpu.make_async_copy(moved, moved, sent.at[index]).wait()
    pltpu.make_async_copy(mixed, mixed, mixed_sem).wait()
    pltpu.make_async_copy(grad_tokens, grad_tokens, grad_sem).wait()


def local(tokens, cotangent, norm1_gain, w_qkv, w_out, pos_bias, norm2_gain, w_up, w_down):
    tile_rows, tile_cols, channels = tokens.shape
    row_devices = lax.axis_size("gy")
    column_devices = lax.axis_size("gx")
    count = row_devices * column_devices
    heads, nodes = pos_bias.shape[:2]
    row_part = tile_rows // row_devices
    extra = row_devices // GRID
    members = GRID // column_devices
    stride = tile_cols // members
    splits = column_devices // row_part
    strip = stride // splits
    per_block = strip // BATCH
    chunks = extra * per_block
    factor = 1.0 / math.sqrt(tile_rows * tile_cols * count)
    plan = (row_devices, column_devices, row_part, extra, members, splits, strip, per_block, heads, factor)
    shape = (tile_rows, members, stride, channels)
    rows = BATCH * MEMBERS
    width = 4 * channels * channels // (16 * count)
    anywhere = pl.BlockSpec(memory_space=pl.ANY)
    vmem = pl.BlockSpec(memory_space=pltpu.VMEM)
    dma = pltpu.SemaphoreType.DMA
    box = (chunks, 2, MEMBERS, BATCH, channels)
    mixed, grad_tokens, grad_qkv, grad_out = pl.pallas_call(
        functools.partial(kernel, plan),
        out_shape=(
            jax.ShapeDtypeStruct(shape, BF16),
            jax.ShapeDtypeStruct(shape, BF16),
            jax.ShapeDtypeStruct((channels, 3 * channels), F32),
            jax.ShapeDtypeStruct((channels, channels), F32),
        ),
        in_specs=[anywhere, anywhere] + [vmem] * 7,
        out_specs=(anywhere, anywhere, vmem, vmem),
        scratch_shapes=[
            pltpu.VMEM(box, BF16),
            pltpu.VMEM(box, BF16),
            pltpu.VMEM((channels, 4 * channels), F32),
            pltpu.VMEM((channels // 128, rows, 128), F32),
            pltpu.VMEM((rows, channels), BF16),
            pltpu.VMEM((rows, channels), BF16),
            pltpu.VMEM((rows, channels), BF16),
            pltpu.VMEM((rows, 3 * channels), BF16),
            pltpu.VMEM((rows, channels), BF16),
            pltpu.VMEM((rows, channels), BF16),
            pltpu.VMEM((rows, 3 * channels), BF16),
            pltpu.VMEM((nodes, heads * nodes), F32),
            pltpu.VMEM((128 * heads // channels * nodes, 128), BF16),
            pltpu.VMEM((column_devices, row_devices, 16, width), BF16),
            pltpu.VMEM((column_devices, row_devices, 16, width), BF16),
            pltpu.VMEM((row_devices, 16, width), BF16),
            pltpu.VMEM((row_devices, 16, width), BF16),
            pltpu.VMEM((16, width), BF16),
            pltpu.VMEM((row_devices, 16, width), BF16),
            pltpu.VMEM((column_devices, row_devices, 16, width), BF16),
            dma((count,)),
            dma((count,)),
            dma((column_devices,)),
            dma((row_devices,)),
            dma((row_devices,)),
            dma((column_devices,)),
            dma((chunks,)),
            dma(()),
            dma(()),
            dma((4,)),
        ],
        compiler_params=pltpu.CompilerParams(
            collective_id=0, has_side_effects=True, vmem_limit_bytes=56 * 1024 * 1024
        ),
    )(
        tokens.reshape(shape),
        cotangent.reshape(shape),
        norm1_gain.reshape(1, channels),
        w_qkv,
        w_out,
        pos_bias.reshape(heads * nodes, nodes),
        norm2_gain.reshape(1, channels),
        w_up,
        w_down,
    )
    return (
        mixed.reshape(tokens.shape),
        grad_tokens.reshape(tokens.shape),
        grad_qkv,
        grad_out,
    )


def solution(mesh):
    placed = (P("gy", "gx", None), P("gy", "gx", None), P(), P(), P(), P(), P(), P(), P())
    return jax.shard_map(
        local,
        mesh=mesh,
        in_specs=placed,
        out_specs=(P("gy", "gx", None), P("gy", "gx", None), P(), P()),
        check_vma=False,
    )
```
